256 devices in a mesh: seq: 128 (over x, z_lo, y, core), dp: 2 (over z_hi).
Axes of the slice: x: 4, y: 4, z: 8 (z_hi: 2, z_lo: 4; z = z_hi * 4 + z_lo), core: 2. Of those that a mesh axis runs over, the one named last changes fastest.
Arguments:
- queries: bfloat16 [2, 32768, 1024], P('dp', 'seq'), may hold values from -8 to 8
- keys: bfloat16 [2, 32768, 1024], P('dp', 'seq'), may hold values from -8 to 8
- values: bfloat16 [2, 32768, 1024], P('dp', 'seq'), may hold values from -6 to 6
- out_grad: bfloat16 [2, 32768, 1024], P('dp', 'seq'), may hold values from -6 to 6
- out_weight: bfloat16 [1024, 1024], replicated, may hold values from -0.1875 to 0.1875
Outputs:
- q_grad: bfloat16 [2, 32768, 1024], P('dp', 'seq')
- k_grad: bfloat16 [2, 32768, 1024], P('dp', 'seq')
- v_grad: bfloat16 [2, 32768, 1024], P('dp', 'seq')
- wo_grad: float32 [1024, 1024], P('seq', 'dp')
The draws below stay inside these ranges and needn't reach their ends.
All inputs are finite; a program needn't handle non-finite values.
Results may differ from the reference program's by a relative error of at most 0.017.
Values may be sent and summed in bfloat16 or wider, within the bound.
A program may use at most 64 MiB of HBM per device.

```python
import jax
import jax.numpy as jnp
from jax import lax

D = 1024
HEAD_DIM = 64
HALF = 128
T_DEV = 256
SEQ_LEN = 32768
UTT = 2


def pair_draw(key):
    base = jax.random.fold_in(key, 7301)
    key_query, key_keys = jax.random.split(base, 2)
    whole_shape = (UTT, SEQ_LEN, D)
    query_part = jax.random.truncated_normal(key_query, -4.0, 4.0, whole_shape, jnp.float32)
    key_part = jax.random.truncated_normal(key_keys, -4.0, 4.0, whole_shape, jnp.float32)
    return (query_part, key_part)


def draw_queries(key, part):
    return pair_draw(key)[0].astype(jnp.bfloat16)


def draw_keys(key, part):
    return pair_draw(key)[1].astype(jnp.bfloat16)


def block_levels(stream_key, dims, shards, least, high):
    factor_of = 1.0
    for dim, shards_of in shards:
        heights = jax.random.uniform(jax.random.fold_in(jax.random.fold_in(stream_key, 6), dim), (shards_of,), jnp.float32, least / len(shards), high / len(shards))
        factor_of = factor_of * jnp.repeat(jnp.exp(heights), dims[dim] // shards_of).reshape((-1,) + (1,) * (len(dims) - 1 - dim))
    return factor_of


def scatter_about(stream_key, shape, scale, reach, cuts=(), kind=jnp.bfloat16):
    array = scale * jax.random.normal(stream_key, shape, jnp.float32)
    if cuts:
        array = array * block_levels(stream_key, shape, cuts, -0.22, 0.18)
    return jnp.clip(array, -reach, reach).astype(kind)


def setup_inputs(seed: int = 0) -> dict:
    key_of = jax.random.split(jax.random.key(seed), 6)
    queries = draw_queries(jax.random.fold_in(key_of[5], 71), 0)
    keys = draw_keys(jax.random.fold_in(key_of[5], 71), 0)
    values = scatter_about(key_of[2], (UTT, SEQ_LEN, D), 1.0, 6.0, ((0, 2), (1, 128)))
    out_grad = scatter_about(key_of[3], (UTT, SEQ_LEN, D), 1.0, 6.0, ((0, 2), (1, 128)))
    out_weight = scatter_about(key_of[4], (D, D), D ** -0.5, 0.1875)
    return dict(queries=queries, keys=keys, values=values, out_grad=out_grad, out_weight=out_weight)


masked_score = -1.0e30


def block_grads(query_rows, key_rows, value_rows, dattn_rows, query_first, key_first):
    count_q = query_rows.shape[0]
    count_k = key_rows.shape[0]
    head_count = D // HEAD_DIM
    scaling = HEAD_DIM ** -0.5
    query_head = query_rows.astype(jnp.float32).reshape(count_q, head_count, HEAD_DIM)
    key_head = key_rows.astype(jnp.float32).reshape(count_k, head_count, HEAD_DIM)
    value_head = value_rows.astype(jnp.float32).reshape(count_k, head_count, HEAD_DIM)
    dattn_head = dattn_rows.astype(jnp.float32).reshape(count_q, head_count, HEAD_DIM)
    query_pos = query_first + jnp.arange(count_q, dtype=jnp.int32)
    key_pos = key_first + jnp.arange(count_k, dtype=jnp.int32)
    inside = (key_pos[None, :] >= query_pos[:, None] - HALF) & (key_pos[None, :] < query_pos[:, None] + HALF)
    inside = inside & (key_pos[None, :] >= 0) & (key_pos[None, :] < SEQ_LEN)
    scores = jnp.einsum("qhd,khd->hqk", query_head, key_head) * scaling
    scores = jnp.where(inside[None], scores, masked_score)
    row_max = jnp.max(scores, axis=-1, keepdims=True)
    log_total = row_max + jnp.log(jnp.sum(jnp.exp(scores - row_max), axis=-1, keepdims=True))
    weights = jnp.exp(scores - log_total)
    weights_bf = lax.optimization_barrier(weights.astype(jnp.bfloat16)).astype(jnp.float32)
    attended = jnp.einsum("hqk,khd->qhd", weights_bf, value_head).astype(jnp.bfloat16)
    attended_wide = lax.optimization_barrier(attended).astype(jnp.float32)
    row_delta = jnp.sum(dattn_head * attended_wide, axis=-1)
    value_grad = jnp.einsum("hqk,qhd->khd", weights_bf, dattn_head)
    dweights = jnp.einsum("qhd,khd->hqk", dattn_head, value_head)
    dscore = (weights * (dweights - row_delta.T[:, :, None])).astype(jnp.bfloat16)
    dscore = lax.optimization_barrier(dscore).astype(jnp.float32)
    query_grad = jnp.einsum("hqk,khd->qhd", dscore, key_head) * scaling
    key_grad = jnp.einsum("hqk,qhd->khd", dscore, query_head) * scaling
    return (attended.reshape(count_q, D), query_grad.reshape(count_q, D),
            key_grad.reshape(count_k, D), value_grad.reshape(count_k, D))


def reference(queries, keys, values, out_grad, out_weight):
    query_list = []
    key_list = []
    value_list = []
    weight_total = jnp.zeros((D, D), jnp.float32)
    blocks = SEQ_LEN // T_DEV
    span = T_DEV + 2 * HALF
    for utterance in range(UTT):
        query_all = queries[utterance]
        grad_all = out_grad[utterance]
        dattn = jnp.dot(grad_all, out_weight.T, preferred_element_type=jnp.float32).astype(jnp.bfloat16)
        keys_pad = jnp.pad(keys[utterance], ((HALF, HALF), (0, 0)))
        values_pad = jnp.pad(values[utterance], ((HALF, HALF), (0, 0)))

        def block_step(accumulators, block_index):
            key_acc, value_acc = accumulators
            start = (block_index * T_DEV).astype(jnp.int32)
            query_rows = lax.dynamic_slice_in_dim(query_all, start, T_DEV, 0)
            dattn_rows = lax.dynamic_slice_in_dim(dattn, start, T_DEV, 0)
            key_rows = lax.dynamic_slice_in_dim(keys_pad, start, span, 0)
            value_rows = lax.dynamic_slice_in_dim(values_pad, start, span, 0)
            attended, query_grad, key_grad, value_grad = block_grads(
                query_rows, key_rows, value_rows, dattn_rows, start, start - HALF)
            key_acc = lax.dynamic_update_slice_in_dim(
                key_acc, lax.dynamic_slice_in_dim(key_acc, start, span, 0) + key_grad, start, 0)
            value_acc = lax.dynamic_update_slice_in_dim(
                value_acc, lax.dynamic_slice_in_dim(value_acc, start, span, 0) + value_grad, start, 0)
            return (key_acc, value_acc), (attended, query_grad.astype(jnp.bfloat16))

        zero_rows = jnp.zeros((SEQ_LEN + 2 * HALF, D), jnp.float32)
        (key_acc, value_acc), (attended_all, query_all_grad) = lax.scan(
            block_step, (zero_rows, zero_rows), jnp.arange(blocks, dtype=jnp.int32))
        attended_all = attended_all.reshape(SEQ_LEN, D)
        weight_total = weight_total + jnp.dot(attended_all.T, grad_all, preferred_element_type=jnp.float32)
        query_list.append(query_all_grad.reshape(SEQ_LEN, D))
        key_list.append(key_acc[HALF:HALF + SEQ_LEN].astype(jnp.bfloat16))
        value_list.append(value_acc[HALF:HALF + SEQ_LEN].astype(jnp.bfloat16))
    wo_grad = weight_total * ((UTT * SEQ_LEN) ** -0.5)
    return (jnp.stack(query_list), jnp.stack(key_list), jnp.stack(value_list), wo_grad)
```

```python
import functools

import jax
import jax.numpy as jnp
from jax import lax
from jax.experimental import pallas as pl
from jax.experimental.pallas import tpu as pltpu
from jax.sharding import PartitionSpec as P

HEAD = 64
HALF = 128
BF = jnp.bfloat16
F32 = jnp.float32
NEG = -1e30
NX, NZ, NY, NC = 4, 4, 4, 2
GROUPS = 4
GW = 256
NT = (((1,), (1,)), ((), ()))
NN = (((1,), (0,)), ((), ()))
SCALE = HEAD ** -0.5


def dot(a, b, dims=NN):
    return lax.dot_general(a, b, dims, preferred_element_type=F32)


def kernel(n_seq, n_dp, q_h, k_h, v_h, g_h, w_h, qo, ko, vo, wo,
           q_s, k_s, v_s, og, w_s, k_t, v_t, q_st, d_st, p_s, a_t, bias,
           part, cs, cr, xs, xr, ysend, yrecv, zs, zr, rs, rr, own,
           load_sem, hsend, hrecv, csend, crecv, xsend, xrecv, ysem, yrsem,
           zsem, zrsem, rsend, rrecv):
    me = lax.axis_index("seq")
    zh = lax.axis_index("dp")
    c = me % NC
    y = (me // NC) % NY
    zl = (me // (NC * NY)) % NZ
    x = me // (NC * NY * NZ)
    rows = 2 * HALF

    def at(x_, z_, y_, c_):
        return ((x_ * NZ + z_) * NY + y_) * NC + c_

    prev = (me + n_seq - 1) % n_seq
    nxt = (me + 1) % n_seq
    mate = at(x, zl, y, 1 - c)
    x_up = at((x + 1) % NX, zl, y, c)
    x_dn = at((x + NX - 1) % NX, zl, y, c)
    x_far = at((x + 1 + (NX - 2) * c) % NX, zl, y, c)
    y_to = [at(x, zl, (y + i) % NY, c) for i in range(1, NY)]
    z_me = zh * NZ + zl
    z_all = [(z_me + i) % (NZ * n_dp) for i in range(1, NZ * n_dp)]
    z_to = [(at(x, z % NZ, y, c), z // NZ) for z in z_all]

    def remote(src, dst, ss, rsem, seq, dp=None):
        return pltpu.make_async_remote_copy(
            src_ref=src, dst_ref=dst, send_sem=ss, recv_sem=rsem,
            device_id={"seq": seq, "dp": zh if dp is None else dp},
            device_id_type=pl.DeviceIdType.MESH)

    barrier = pltpu.get_barrier_semaphore()
    partners = [(prev, zh), (nxt, zh), (x_up, zh), (x_dn, zh)]
    partners += [(s, zh) for s in y_to] + z_to
    for s, d in partners:
        pl.semaphore_signal(barrier, inc=1, device_id={"seq": s, "dp": d},
                            device_id_type=pl.DeviceIdType.MESH)

    loads = [pltpu.make_async_copy(g_h, og, load_sem.at[0]),
             pltpu.make_async_copy(w_h, w_s, load_sem.at[1])]
    for g in range(GROUPS):
        cols = pl.ds(g * GW, GW)
        loads.append(pltpu.make_async_copy(q_h.at[:, cols], q_s.at[g], load_sem.at[2 + g]))
        loads.append(pltpu.make_async_copy(
            k_h.at[:, cols], k_s.at[g, pl.ds(HALF, rows)], load_sem.at[6 + g]))
        loads.append(pltpu.make_async_copy(
            v_h.at[:, cols], v_s.at[g, pl.ds(HALF, rows)], load_sem.at[10 + g]))
    for cp in loads:
        cp.start()

    pl.semaphore_wait(barrier, len(partners))

    order = [(x + 2) % NX, (x + 1) % NX, (x + 3) % NX, x]
    halos = []
    for g in order:
        cols = pl.ds(pl.multiple_of(g * GW, GW), GW)
        mine = []
        for a, (src, dst) in enumerate(((k_h, k_s), (v_h, v_s))):
            mine.append(remote(src.at[pl.ds(HALF, HALF), cols], dst.at[g, pl.ds(0, HALF)],
                               hsend.at[a, 0, g], hrecv.at[a, 0, g], nxt))
            mine.append(remote(src.at[pl.ds(0, HALF), cols], dst.at[g, pl.ds(3 * HALF, HALF)],
                               hsend.at[a, 1, g], hrecv.at[a, 1, g], prev))
        for cp in mine:
            cp.start()
        halos.append(mine)

    for cp in loads:
        cp.wait()

    row_j = lax.broadcasted_iota(jnp.int32, (HALF, 2 * HALF), 0)
    col_i = lax.broadcasted_iota(jnp.int32, (HALF, 2 * HALF), 1) % HALF
    keep = row_j >= col_i
    first_dev = jnp.where(me == 0, NEG, 0.0).astype(F32)
    last_dev = jnp.where(me == n_seq - 1, NEG, 0.0).astype(F32)
    bias[0] = jnp.where(keep, first_dev, 0.0)
    bias[1] = jnp.where(keep, 0.0, last_dev)
    lane = lax.broadcasted_iota(jnp.int32, (HALF, HALF), 1)
    left = lane < HEAD

    def stacked(t):
        zero = jnp.zeros_like(t)
        return jnp.concatenate([jnp.where(left, t, zero), jnp.where(left, zero, t)], axis=0)

    for g in range(GROUPS):
        dattn = dot(og[...], w_s[g * GW:(g + 1) * GW, :], NT).astype(BF).astype(F32)
        for p in range(2):
            for b in range(2):
                rb, cb = b * HALF, p * HALF
                d_st[g, p, b] = stacked(dattn[rb:rb + HALF, cb:cb + HALF]).astype(BF)
                qq = q_s[g, rb:rb + HALF, cb:cb + HALF].astype(F32) * SCALE
                q_st[g, p, b] = stacked(qq).astype(BF)
            k_t[g, p, :, HALF:3 * HALF] = k_s[g, HALF:3 * HALF, cb:cb + HALF].T
            v_t[g, p, :, HALF:3 * HALF] = v_s[g, HALF:3 * HALF, cb:cb + HALF].T

    def diagonal(t):
        return jnp.concatenate([t[:HEAD, :HALF], t[HEAD:, HALF:]], axis=0)

    def forward(g):
        for p in range(2):
            cb = p * HALF
            for e in (0, 3 * HALF):
                k_t[g, p, :, e:e + HALF] = k_s[g, e:e + HALF, cb:cb + HALF].T
                v_t[g, p, :, e:e + HALF] = v_s[g, e:e + HALF, cb:cb + HALF].T
            for b in range(2):
                r0 = b * HALF
                sc = dot(k_s[g, r0:r0 + 3 * HALF, cb:cb + HALF], q_st[g, p, b], NT)
                mid = sc[HALF:2 * HALF]
                mix = jnp.where(keep, sc[:HALF], sc[2 * HALF:]) + bias[b]
                top = jnp.maximum(jnp.max(mid, axis=0, keepdims=True),
                                  jnp.max(mix, axis=0, keepdims=True))
                mid = jnp.exp(mid - top)
                mix = jnp.exp(mix - top)
                total = jnp.sum(mid, axis=0, keepdims=True) + jnp.sum(mix, axis=0, keepdims=True)
                inv = 1.0 / total
                mid = mid * inv
                mix = mix * inv
                pr = jnp.concatenate(
                    [jnp.where(keep, mix, 0.0), mid, jnp.where(keep, 0.0, mix)], axis=0).astype(BF)
                p_s[g, p, b] = pr
                att = dot(v_t[g, p, :, r0:r0 + 3 * HALF], pr)
                a_t[cb:cb + HALF, r0:r0 + HALF] = diagonal(att).astype(BF)

    def project(g, slot):
        for h in range(NZ):
            r = dot(a_t[h * HEAD:(h + 1) * HEAD, :], og[...])
            part[slot, h * 8:(h + 1) * 8] = r.reshape(8, 8, r.shape[1])
        for yy in range(NY):
            for h in range(0, NZ, 2):
                t = jnp.concatenate([part[slot, h * 8 + yy * 2 + (1 - c)],
                                     part[slot, (h + 1) * 8 + yy * 2 + (1 - c)]], axis=0)
                r0 = yy * 32 + h * 8
                cs[slot, r0:r0 + 16] = t.astype(BF)
        cp = remote(cs.at[slot], cr.at[slot], csend.at[slot], crecv.at[slot], mate)
        cp.start()
        return cp

    def summed(slot, yy, h):
        r0 = yy * 32 + h * 8
        t = jnp.concatenate([part[slot, h * 8 + yy * 2 + c],
                             part[slot, (h + 1) * 8 + yy * 2 + c]], axis=0)
        return t + cr[slot, r0:r0 + 16].astype(F32)

    pieces = [(yy, h) for yy in range(NY) for h in range(0, NZ, 2)]

    def x_fill(slot, extra):
        for yy, h in pieces:
            r0 = yy * 32 + h * 8
            t = summed(slot, yy, h)
            if extra:
                t = t + xr[0, r0:r0 + 16].astype(F32)
            xs[slot, r0:r0 + 16] = t.astype(BF)

    far = remote(xs.at[0], xr.at[0], xsend.at[0], xrecv.at[0], x_far)
    up = remote(xs.at[1], xr.at[1], xsend.at[1], xrecv.at[1], x_up)
    down = remote(xs.at[2], xr.at[2], xsend.at[2], xrecv.at[2], x_dn)

    def x_send(slot):
        cores[slot].wait_recv()
        if slot == 0:
            x_fill(0, False)
            far.start()
            return
        adds = c == (0 if slot == 1 else 1)

        @pl.when(adds)
        def _():
            far.wait_recv()
            x_fill(slot, True)

        @pl.when(jnp.logical_not(adds))
        def _():
            x_fill(slot, False)

        (up if slot == 1 else down).start()

    cores = []
    for i, g in enumerate(order):
        for cp in halos[i]:
            cp.wait_recv()
        forward(g)
        cores.append(project(g, i))
        if i >= 1:
            x_send(i - 1)

    def backward(g):
        for p in range(2):
            cb = p * HALF
            dks, dvs = [], []
            for b in range(2):
                r0 = b * HALF
                dp = dot(v_s[g, r0:r0 + 3 * HALF, cb:cb + HALF], d_st[g, p, b], NT)
                pr = p_s[g, p, b]
                prf = pr.astype(F32)
                t = prf * dp
                delta = jnp.sum(t, axis=0, keepdims=True)
                ds = (t - prf * delta).astype(BF)
                dq = diagonal(dot(k_t[g, p, :, r0:r0 + 3 * HALF], ds)) * SCALE
                qo[r0:r0 + HALF, pl.ds(pl.multiple_of(g * GW + cb, HALF), HALF)] = dq.T.astype(BF)
                dks.append(dot(ds, q_st[g, p, b]))
                dvs.append(dot(pr, d_st[g, p, b]))
            for a, t in enumerate((dks, dvs)):
                rs[0, g, a, :, cb:cb + HALF] = t[0][:HALF].astype(BF)
                rs[1, g, a, :, cb:cb + HALF] = t[1][2 * HALF:].astype(BF)
                own[g, a, :HALF, cb:cb + HALF] = t[0][HALF:2 * HALF] + t[1][:HALF]
                own[g, a, HALF:, cb:cb + HALF] = t[0][2 * HALF:] + t[1][HALF:2 * HALF]
        lo = remote(rs.at[0, g], rr.at[0, g], rsend.at[0, g], rrecv.at[0, g], prev)
        hi = remote(rs.at[1, g], rr.at[1, g], rsend.at[1, g], rrecv.at[1, g], nxt)
        lo.start()
        hi.start()
        return lo, hi

    def finish(i):
        g = order[i]
        for cp in rims[i]:
            cp.wait_recv()
        cols = pl.ds(pl.multiple_of(g * GW, GW), GW)
        for a, out in enumerate((ko, vo)):
            out[:HALF, cols] = (own[g, a, :HALF] + rr[1, g, a].astype(F32)).astype(BF)
            out[HALF:, cols] = (own[g, a, HALF:] + rr[0, g, a].astype(F32)).astype(BF)

    y_copies = [remote(ysend.at[(y + i) % NY], yrecv.at[i - 1], ysem.at[i - 1], yrsem.at[i - 1],
                       y_to[i - 1]) for i in range(1, NY)]
    z_copies = [remote(zs.at[z], zr.at[i], zsem.at[i], zrsem.at[i], z_to[i][0], z_to[i][1])
                for i, z in enumerate(z_all)]

    def y_stage():
        cores[3].wait_recv()
        up.wait_recv()
        down.wait_recv()
        for yy, h in pieces:
            r0 = yy * 32 + h * 8
            t = (summed(3, yy, h) + xr[1, r0:r0 + 16].astype(F32)
                 + xr[2, r0:r0 + 16].astype(F32))
            ysend[yy, h * 8:h * 8 + 16] = t.astype(BF)
            part[0, h * 4 + yy] = t[:8]
            part[0, (h + 1) * 4 + yy] = t[8:]
        for cp in y_copies:
            cp.start()

    def z_stage():
        for cp in y_copies:
            cp.wait_recv()
        half = og.shape[1] // n_dp
        got = yrecv[0].astype(F32) + yrecv[1].astype(F32) + yrecv[2].astype(F32)
        for h in range(NZ):
            t = part[0, h * 4 + y] + got[h * 8:(h + 1) * 8]
            for d in range(n_dp):
                zs[d * NZ + h] = t[:, d * half:(d + 1) * half]
        for cp in z_copies:
            cp.start()

    def z_finish():
        for cp in z_copies:
            cp.wait_recv()
        t = zs[z_me]
        for i in range(len(z_copies)):
            t = t + zr[i]
        wo[...] = t * ((rows * n_seq * n_dp) ** -0.5)

    rims = []
    for i, g in enumerate(order):
        rims.append(backward(g))
        if i == 0:
            y_stage()
        elif i == 1:
            z_stage()
        elif i == 2:
            finish(0)
        else:
            z_finish()
            finish(1)
    finish(2)
    finish(3)

    for mine in halos:
        for cp in mine:
            cp.wait_send()
    for cp in cores + [far, up, down] + y_copies + z_copies:
        cp.wait_send()

    for mine in rims:
        for cp in mine:
            cp.wait_send()


def on_device(n_seq, n_dp, queries, keys, values, out_grad, out_weight):
    rows, width = queries.shape[1:]
    half = width // n_dp
    vm = pltpu.VMEM
    dma = pltpu.SemaphoreType.DMA
    nz = NZ * n_dp
    anyspec = pl.BlockSpec(memory_space=pl.ANY)
    vspec = pl.BlockSpec(memory_space=pltpu.VMEM)
    scratch = [
        vm((GROUPS, rows, GW), BF), vm((GROUPS, 4 * HALF, GW), BF), vm((GROUPS, 4 * HALF, GW), BF),
        vm((rows, width), BF), vm((width, width), BF),
        vm((GROUPS, 2, HALF, 4 * HALF), BF), vm((GROUPS, 2, HALF, 4 * HALF), BF),
        vm((GROUPS, 2, 2, 2 * HALF, HALF), BF), vm((GROUPS, 2, 2, 2 * HALF, HALF), BF),
        vm((GROUPS, 2, 2, 3 * HALF, 2 * HALF), BF), vm((GW, rows), BF), vm((2, HALF, 2 * HALF), F32),
        vm((4, 32, 8, width), F32), vm((4, HALF, width), BF), vm((4, HALF, width), BF),
        vm((3, HALF, width), BF), vm((3, HALF, width), BF),
        vm((NY, 32, width), BF), vm((NY - 1, 32, width), BF),
        vm((nz, 8, half), F32), vm((nz - 1, 8, half), F32),
        vm((2, GROUPS, 2, HALF, GW), BF), vm((2, GROUPS, 2, HALF, GW), BF),
        vm((GROUPS, 2, rows, GW), F32),
        dma((14,)), dma((2, 2, GROUPS)), dma((2, 2, GROUPS)), dma((4,)), dma((4,)),
        dma((3,)), dma((3,)), dma((NY - 1,)), dma((NY - 1,)), dma((nz - 1,)), dma((nz - 1,)),
        dma((2, GROUPS)), dma((2, GROUPS)),
    ]
    sds = jax.ShapeDtypeStruct
    qg, kg, vg, wg = pl.pallas_call(
        functools.partial(kernel, n_seq, n_dp),
        out_shape=[sds((rows, width), BF)] * 3 + [sds((8, half), F32)],
        in_specs=[anyspec] * 5,
        out_specs=[vspec] * 4,
        scratch_shapes=scratch,
        compiler_params=pltpu.CompilerParams(
            collective_id=0, has_side_effects=True, vmem_limit_bytes=48 * 1024 * 1024),
    )(queries[0], keys[0], values[0], out_grad[0], out_weight)
    return qg[None], kg[None], vg[None], wg


def solution(mesh):
    n_seq, n_dp = mesh.shape["seq"], mesh.shape["dp"]
    rows = P("dp", "seq", None)
    return jax.shard_map(
        functools.partial(on_device, n_seq, n_dp),
        mesh=mesh,
        in_specs=(rows, rows, rows, rows, P()),
        out_specs=(rows, rows, rows, P("seq", "dp")),
        check_vma=False,
    )
```

```python
import functools

import jax
import jax.numpy as jnp
from jax import lax
from jax.experimental import pallas as pl
from jax.experimental.pallas import tpu as pltpu
from jax.sharding import PartitionSpec as P

HEAD = 64
HALF = 128
BF = jnp.bfloat16
F32 = jnp.float32
NEG = -1e30
NX, NZ, NY, NC = 4, 4, 4, 2
GROUPS = 4
GW = 256
NT = (((1,), (1,)), ((), ()))
NN = (((1,), (0,)), ((), ()))
SCALE = HEAD ** -0.5


def dot(a, b, dims=NN):
    return lax.dot_general(a, b, dims, preferred_element_type=F32)


def kernel(n_seq, n_dp, q_h, k_h, v_h, g_h, w_h, qo, ko, vo, wo,
           q_s, k_s, v_s, og, w_s, k_t, v_t, q_st, d_st, p_s, a_t, bias,
           part, cs, cr, xs, xr, ysend, yrecv, y_own, zs, zr, z_own, rs, rr, own,
           load_sem, hsend, hrecv, csend, crecv, xsend, xrecv, ysem, yrsem,
           zsem, zrsem, rsend, rrecv):
    me = lax.axis_index("seq")
    zh = lax.axis_index("dp")
    c = me % NC
    y = (me // NC) % NY
    zl = (me // (NC * NY)) % NZ
    x = me // (NC * NY * NZ)
    rows = 2 * HALF

    def at(x_, z_, y_, c_):
        return ((x_ * NZ + z_) * NY + y_) * NC + c_

    prev = (me + n_seq - 1) % n_seq
    nxt = (me + 1) % n_seq
    mate = at(x, zl, y, 1 - c)
    x_up = at((x + 1) % NX, zl, y, c)
    x_dn = at((x + NX - 1) % NX, zl, y, c)
    x_far = at((x + 1 + (NX - 2) * c) % NX, zl, y, c)
    y_to = [at(x, zl, (y + i) % NY, c) for i in range(1, NY)]
    z_me = zh * NZ + zl
    z_all = [(z_me + i) % (NZ * n_dp) for i in range(1, NZ * n_dp)]
    z_to = [(at(x, z % NZ, y, c), z // NZ) for z in z_all]

    def remote(src, dst, ss, rsem, seq, dp=None):
        return pltpu.make_async_remote_copy(
            src_ref=src, dst_ref=dst, send_sem=ss, recv_sem=rsem,
            device_id={"seq": seq, "dp": zh if dp is None else dp},
            device_id_type=pl.DeviceIdType.MESH)

    barrier = pltpu.get_barrier_semaphore()
    partners = [(prev, zh), (nxt, zh), (x_up, zh), (x_dn, zh)]
    partners += [(s, zh) for s in y_to] + z_to
    for s, d in partners:
        pl.semaphore_signal(barrier, inc=1, device_id={"seq": s, "dp": d},
                            device_id_type=pl.DeviceIdType.MESH)

    loads = [pltpu.make_async_copy(g_h, og, load_sem.at[0]),
             pltpu.make_async_copy(w_h, w_s, load_sem.at[1])]
    for g in range(GROUPS):
        cols = pl.ds(g * GW, GW)
        loads.append(pltpu.make_async_copy(q_h.at[:, cols], q_s.at[g], load_sem.at[2 + g]))
        loads.append(pltpu.make_async_copy(
            k_h.at[:, cols], k_s.at[g, pl.ds(HALF, rows)], load_sem.at[6 + g]))
        loads.append(pltpu.make_async_copy(
            v_h.at[:, cols], v_s.at[g, pl.ds(HALF, rows)], load_sem.at[10 + g]))
    for cp in loads:
        cp.start()

    pl.semaphore_wait(barrier, len(partners))

    def order_of(x_):
        return [(x_ + 2) % NX, (x_ + 1) % NX, (x_ + 3) % NX, x_]

    def halo(a, side, g):
        src, dst = ((k_h, k_s), (v_h, v_s))[a]
        cols = pl.ds(pl.multiple_of(g * GW, GW), GW)
        return remote(src.at[pl.ds(HALF * (1 - side), HALF), cols],
                      dst.at[g, pl.ds(3 * HALF * side, HALF)],
                      hsend.at[a, side, g], hrecv.at[a, side, g], (nxt, prev)[side])

    order = order_of(x)
    per_x = NZ * NY * NC
    for g_nxt, g_prev in zip(order_of(nxt // per_x), order_of(prev // per_x)):
        for a in range(2):
            halo(a, 0, g_nxt).start()
            halo(a, 1, g_prev).start()
    halos = [[halo(a, side, g) for a in range(2) for side in range(2)] for g in order]

    for cp in loads:
        cp.wait()

    row_j = lax.broadcasted_iota(jnp.int32, (HALF, 2 * HALF), 0)
    col_i = lax.broadcasted_iota(jnp.int32, (HALF, 2 * HALF), 1) % HALF
    keep = row_j >= col_i
    first_dev = jnp.where(me == 0, NEG, 0.0).astype(F32)
    last_dev = jnp.where(me == n_seq - 1, NEG, 0.0).astype(F32)
    bias[0] = jnp.where(keep, first_dev, 0.0)
    bias[1] = jnp.where(keep, 0.0, last_dev)
    lane = lax.broadcasted_iota(jnp.int32, (HALF, HALF), 1)
    left = lane < HEAD

    def stacked(t):
        zero = jnp.zeros_like(t)
        return jnp.concatenate([jnp.where(left, t, zero), jnp.where(left, zero, t)], axis=0)

    for g in range(GROUPS):
        dattn = dot(og[...], w_s[g * GW:(g + 1) * GW, :], NT).astype(BF).astype(F32)
        for p in range(2):
            cb = p * HALF
            for b in range(2):
                rb = b * HALF
                d_st[g, p, b] = stacked(dattn[rb:rb + HALF, cb:cb + HALF]).astype(BF)
                qq = q_s[g, rb:rb + HALF, cb:cb + HALF].astype(F32) * SCALE
                q_st[g, p, b] = stacked(qq).astype(BF)
            k_t[g, p, :, HALF:3 * HALF] = k_s[g, HALF:3 * HALF, cb:cb + HALF].T
            v_t[g, p, :, HALF:3 * HALF] = v_s[g, HALF:3 * HALF, cb:cb + HALF].T

    def diagonal(t):
        return jnp.concatenate([t[:HEAD, :HALF], t[HEAD:, HALF:]], axis=0)

    def forward(g, p):
        cb = p * HALF
        for e in (0, 3 * HALF):
            v_t[g, p, :, e:e + HALF] = v_s[g, e:e + HALF, cb:cb + HALF].T
        for b in range(2):
            r0 = b * HALF
            sc = dot(k_s[g, r0:r0 + 3 * HALF, cb:cb + HALF], q_st[g, p, b], NT)
            mid = sc[HALF:2 * HALF]
            mix = jnp.where(keep, sc[:HALF], sc[2 * HALF:]) + bias[b]
            top = jnp.maximum(jnp.max(mid, axis=0, keepdims=True),
                              jnp.max(mix, axis=0, keepdims=True))
            mid = jnp.exp(mid - top)
            mix = jnp.exp(mix - top)
            total = jnp.sum(mid, axis=0, keepdims=True) + jnp.sum(mix, axis=0, keepdims=True)
            inv = 1.0 / total
            mid = mid * inv
            mix = mix * inv
            pr = jnp.concatenate(
                [jnp.where(keep, mix, 0.0), mid, jnp.where(keep, 0.0, mix)], axis=0).astype(BF)
            p_s[g, p, b] = pr
            att = dot(v_t[g, p, :, r0:r0 + 3 * HALF], pr)
            a_t[:, r0:r0 + HALF] = diagonal(att).astype(BF)

    def project(slot):
        r = dot(a_t[...], og[...])
        part[slot] = r.reshape(16, 8, r.shape[1])
        for yy in range(NY):
            t = jnp.concatenate([part[slot, yy * 2 + (1 - c)],
                                 part[slot, 8 + yy * 2 + (1 - c)]], axis=0)
            cs[slot, yy * 16:yy * 16 + 16] = t.astype(BF)
        cp = remote(cs.at[slot], cr.at[slot], csend.at[slot], crecv.at[slot], mate)
        cp.start()
        return cp

    def summed(slot, yy):
        t = jnp.concatenate([part[slot, yy * 2 + c], part[slot, 8 + yy * 2 + c]], axis=0)
        return t + cr[slot, yy * 16:yy * 16 + 16].astype(F32)

    x_dest = [x_far, x_far, x_up, x_dn, x_up, x_dn]
    x_copies = [remote(xs.at[k], xr.at[k], xsend.at[k], xrecv.at[k], x_dest[k]) for k in range(6)]

    def x_fill(slot, extra):
        for yy in range(NY):
            t = summed(slot, yy)
            if extra is not None:
                t = t + xr[extra, yy * 16:yy * 16 + 16].astype(F32)
            xs[slot, yy * 16:yy * 16 + 16] = t.astype(BF)

    def x_send(slot):
        cores[slot].wait_recv()
        if slot < 2:
            x_fill(slot, None)
        else:
            far = 0 if slot < 4 else 1
            adds = c == slot % 2

            @pl.when(adds)
            def _():
                x_copies[far].wait_recv()
                x_fill(slot, far)

            @pl.when(jnp.logical_not(adds))
            def _():
                x_fill(slot, None)

        x_copies[slot].start()

    cores = []
    g_far, g_up, g_dn, g_own = order
    steps = [(0, g_far, 0), (0, g_far, 1), (1, g_up, 0), (2, g_dn, 0),
             (1, g_up, 1), (2, g_dn, 1), (3, g_own, 0), (3, g_own, 1)]
    x_after = {1: [0], 2: [1], 4: [2, 3], 5: [4], 6: [5]}
    for i, (place, g, p) in enumerate(steps):
        if i in (0, 2, 3, 6):
            for cp in halos[place]:
                cp.wait_recv()
        forward(g, p)
        cores.append(project(i))
        for slot in x_after.get(i, []):
            x_send(slot)

    def backward(g, p):
        cb = p * HALF
        for e in (0, 3 * HALF):
            k_t[g, p, :, e:e + HALF] = k_s[g, e:e + HALF, cb:cb + HALF].T
        dks, dvs = [], []
        for b in range(2):
            r0 = b * HALF
            dp = dot(v_s[g, r0:r0 + 3 * HALF, cb:cb + HALF], d_st[g, p, b], NT)
            pr = p_s[g, p, b]
            prf = pr.astype(F32)
            t = prf * dp
            delta = jnp.sum(t, axis=0, keepdims=True)
            ds = (t - prf * delta).astype(BF)
            dks.append(dot(ds, q_st[g, p, b]))
            dvs.append(dot(pr, d_st[g, p, b]))
            dq = diagonal(dot(k_t[g, p, :, r0:r0 + 3 * HALF], ds)) * SCALE
            qo[r0:r0 + HALF, g * GW + cb:g * GW + cb + HALF] = dq.T.astype(BF)
        j = g * 2 + p
        for a, t in enumerate((dks, dvs)):
            rs[0, j, a] = t[0][:HALF].astype(BF)
            rs[1, j, a] = t[1][2 * HALF:].astype(BF)
            own[j, a, :HALF] = t[0][HALF:2 * HALF] + t[1][:HALF]
            own[j, a, HALF:] = t[0][2 * HALF:] + t[1][HALF:2 * HALF]
        lo = remote(rs.at[0, j], rr.at[0, j], rsend.at[0, j], rrecv.at[0, j], prev)
        hi = remote(rs.at[1, j], rr.at[1, j], rsend.at[1, j], rrecv.at[1, j], nxt)
        lo.start()
        hi.start()
        return lo, hi

    def finish(j):
        for cp in rims[j]:
            cp.wait_recv()
        for a, out in enumerate((ko, vo)):
            cols = slice(j * HALF, (j + 1) * HALF)
            out[:HALF, cols] = (own[j, a, :HALF] + rr[1, j, a].astype(F32)).astype(BF)
            out[HALF:, cols] = (own[j, a, HALF:] + rr[0, j, a].astype(F32)).astype(BF)

    y_copies = [[remote(ysend.at[p, (y + i) % NY], yrecv.at[p, i - 1], ysem.at[p, i - 1],
                        yrsem.at[p, i - 1], y_to[i - 1]) for i in range(1, NY)] for p in range(2)]
    z_copies = [remote(zs.at[z], zr.at[i], zsem.at[i], zrsem.at[i], z_to[i][0], z_to[i][1])
                for i, z in enumerate(z_all)]
    quarter = og.shape[1] // (2 * n_dp)

    def y_stage(p):
        cores[6 + p].wait_recv()
        x_copies[2 + 2 * p].wait_recv()
        x_copies[3 + 2 * p].wait_recv()
        for yy in range(NY):
            r0 = yy * 16
            t = (summed(6 + p, yy) + xr[2 + 2 * p, r0:r0 + 16].astype(F32)
                 + xr[3 + 2 * p, r0:r0 + 16].astype(F32))
            ysend[p, yy] = t.astype(BF)
            y_own[p, yy] = t
        for cp in y_copies[p]:
            cp.start()

    def z_stage():
        for p in range(2):
            for cp in y_copies[p]:
                cp.wait_recv()
        for p in range(2):
            t = y_own[p, y]
            for i in range(NY - 1):
                t = t + yrecv[p, i].astype(F32)
            for h in range(2):
                for d in range(n_dp):
                    u = t[h * 8:h * 8 + 8, d * 2 * quarter:(d + 1) * 2 * quarter]
                    u = jnp.concatenate([u[:, :quarter], u[:, quarter:]], axis=0)
                    z_own[d * NZ + p * 2 + h] = u
                    zs[d * NZ + p * 2 + h] = u.astype(BF)
        for cp in z_copies:
            cp.start()

    def z_finish():
        for cp in z_copies:
            cp.wait_recv()
        t = z_own[z_me]
        for i in range(len(z_copies)):
            t = t + zr[i].astype(F32)
        t = t * ((rows * n_seq * n_dp) ** -0.5)
        wo[:, :quarter] = t[:8]
        wo[:, quarter:] = t[8:]

    rims = []
    for g in range(GROUPS):
        for p in range(2):
            rims.append(backward(g, p))
            if len(rims) == 3:
                y_stage(0)
            elif len(rims) == 5:
                y_stage(1)
    z_stage()
    for j in range(2 * GROUPS):
        finish(j)
    z_finish()

    for g_nxt, g_prev in zip(order_of(nxt // per_x), order_of(prev // per_x)):
        for a in range(2):
            halo(a, 0, g_nxt).wait_send()
            halo(a, 1, g_prev).wait_send()
    for cp in cores + x_copies + y_copies[0] + y_copies[1] + z_copies:
        cp.wait_send()
    for pair in rims:
        for cp in pair:
            cp.wait_send()


def on_device(n_seq, n_dp, queries, keys, values, out_grad, out_weight):
    rows, width = queries.shape[1:]
    half = width // n_dp
    vm = pltpu.VMEM
    dma = pltpu.SemaphoreType.DMA
    nz = NZ * n_dp
    anyspec = pl.BlockSpec(memory_space=pltpu.HBM)
    vspec = pl.BlockSpec(memory_space=pltpu.VMEM)
    scratch = [
        vm((GROUPS, rows, GW), BF), vm((GROUPS, 4 * HALF, GW), BF), vm((GROUPS, 4 * HALF, GW), BF),
        vm((rows, width), BF), vm((width, width), BF),
        vm((GROUPS, 2, HALF, 4 * HALF), BF), vm((GROUPS, 2, HALF, 4 * HALF), BF),
        vm((GROUPS, 2, 2, 2 * HALF, HALF), BF), vm((GROUPS, 2, 2, 2 * HALF, HALF), BF),
        vm((GROUPS, 2, 2, 3 * HALF, 2 * HALF), BF), vm((HALF, rows), BF), vm((2, HALF, 2 * HALF), F32),
        vm((8, 16, 8, width), F32), vm((8, HEAD, width), BF), vm((8, HEAD, width), BF),
        vm((6, HEAD, width), BF), vm((6, HEAD, width), BF),
        vm((2, NY, 16, width), BF), vm((2, NY - 1, 16, width), BF), vm((2, NY, 16, width), F32),
        vm((nz, 16, half // 2), BF), vm((nz - 1, 16, half // 2), BF), vm((nz, 16, half // 2), F32),
        vm((2, 8, 2, HALF, HALF), BF), vm((2, 8, 2, HALF, HALF), BF),
        vm((8, 2, rows, HALF), F32),
        dma((14,)), dma((2, 2, GROUPS)), dma((2, 2, GROUPS)), dma((8,)), dma((8,)),
        dma((6,)), dma((6,)), dma((2, NY - 1)), dma((2, NY - 1)), dma((nz - 1,)), dma((nz - 1,)),
        dma((2, 8)), dma((2, 8)),
    ]
    sds = jax.ShapeDtypeStruct
    outs = [sds((rows, width), BF)] * 3 + [sds((8, half), F32)]
    qg, kg, vg, wg = pl.pallas_call(
        functools.partial(kernel, n_seq, n_dp),
        out_shape=outs,
        in_specs=[anyspec] * 5,
        out_specs=[vspec] * 4,
        scratch_shapes=scratch,
        compiler_params=pltpu.CompilerParams(
            collective_id=0, has_side_effects=True, vmem_limit_bytes=48 * 1024 * 1024),
    )(*[pltpu.with_memory_space_constraint(t, pltpu.HBM)
        for t in (queries[0], keys[0], values[0], out_grad[0], out_weight)])
    return qg[None], kg[None], vg[None], wg


def solution(mesh):
    n_seq, n_dp = mesh.shape["seq"], mesh.shape["dp"]
    rows = P("dp", "seq", None)
    return jax.shard_map(
        functools.partial(on_device, n_seq, n_dp),
        mesh=mesh,
        in_specs=(rows, rows, rows, rows, P()),
        out_specs=(rows, rows, rows, P("seq", "dp")),
        check_vma=False,
    )
```

```python
import functools

import jax
import jax.numpy as jnp
from jax import lax
from jax.experimental import pallas as pl
from jax.experimental.pallas import tpu as pltpu
from jax.sharding import PartitionSpec as P

HEAD = 64
HALF = 128
BF = jnp.bfloat16
F32 = jnp.float32
NEG = -1e30
NX, NZ, NY, NC = 4, 4, 4, 2
GROUPS = 4
GW = 256
NT = (((1,), (1,)), ((), ()))
NN = (((1,), (0,)), ((), ()))
SCALE = HEAD ** -0.5


def dot(a, b, dims=NN):
    return lax.dot_general(a, b, dims, preferred_element_type=F32)


def kernel(n_seq, n_dp, q_h, k_h, v_h, g_h, w_h, all_o, wo,
           q_s, k_s, v_s, og, w_s, k_t, v_t, q_st, d_st, p_s, a_t, bias,
           part, cs, cr, xs, xr, ysend, yrecv, y_own, zs, zr, z_own, rs, rr, own,
           load_sem, hsend, hrecv, csend, crecv, xsend, xrecv, ysem, yrsem,
           zsem, zrsem, rsend, rrecv):
    me = lax.axis_index("seq")
    zh = lax.axis_index("dp")
    c = me % NC
    y = (me // NC) % NY
    zl = (me // (NC * NY)) % NZ
    x = me // (NC * NY * NZ)
    rows = 2 * HALF
    qo, ko, vo = all_o.at[0], all_o.at[1], all_o.at[2]

    def at(x_, z_, y_, c_):
        return ((x_ * NZ + z_) * NY + y_) * NC + c_

    prev = (me + n_seq - 1) % n_seq
    nxt = (me + 1) % n_seq
    mate = at(x, zl, y, 1 - c)
    x_up = at((x + 1) % NX, zl, y, c)
    x_dn = at((x + NX - 1) % NX, zl, y, c)
    x_far = at((x + 1 + (NX - 2) * c) % NX, zl, y, c)
    y_to = [at(x, zl, (y + i) % NY, c) for i in range(1, NY)]
    z_me = zh * NZ + zl
    z_all = [(z_me + i) % (NZ * n_dp) for i in range(1, NZ * n_dp)]
    z_to = [(at(x, z % NZ, y, c), z // NZ) for z in z_all]

    def remote(src, dst, ss, rsem, seq, dp=None):
        return pltpu.make_async_remote_copy(
            src_ref=src, dst_ref=dst, send_sem=ss, recv_sem=rsem,
            device_id={"seq": seq, "dp": zh if dp is None else dp},
            device_id_type=pl.DeviceIdType.MESH)

    barrier = pltpu.get_barrier_semaphore()
    partners = [(prev, zh), (nxt, zh), (x_up, zh), (x_dn, zh)]
    partners += [(s, zh) for s in y_to] + z_to
    for s, d in partners:
        pl.semaphore_signal(barrier, inc=1, device_id={"seq": s, "dp": d},
                            device_id_type=pl.DeviceIdType.MESH)

    def order_of(x_):
        return [(x_ + 2) % NX, (x_ + 1) % NX, (x_ + 3) % NX, x_]

    order = order_of(x)

    def loads(g):
        cols = pl.ds(pl.multiple_of(g * GW, GW), GW)
        mid = pl.ds(HALF, rows)
        return [pltpu.make_async_copy(q_h.at[:, cols], q_s.at[g], load_sem.at[2 + g]),
                pltpu.make_async_copy(k_h.at[:, cols], k_s.at[g, mid], load_sem.at[6 + g]),
                pltpu.make_async_copy(v_h.at[:, cols], v_s.at[g, mid], load_sem.at[10 + g])]

    load_og = pltpu.make_async_copy(g_h, og, load_sem.at[0])
    load_w = pltpu.make_async_copy(w_h, w_s, load_sem.at[1])
    for i, g in enumerate(order):
        for cp in loads(g):
            cp.start()
        if i == 0:
            load_og.start()
    load_w.start()

    pl.semaphore_wait(barrier, len(partners))

    away = (me + n_seq - 1 + 2 * c) % n_seq
    sides = ((mate, 1 - c), (away, c))

    def halo(a, side, g):
        buf = (k_s, v_s)[a]
        dev, b = sides[side]
        return remote(buf.at[g, pl.ds(pl.multiple_of(HALF * (1 + b), HALF), HALF)],
                      buf.at[g, pl.ds(pl.multiple_of(3 * HALF * (1 - b), HALF), HALF)],
                      hsend.at[a, side, g], hrecv.at[a, side, g], dev)

    away_order = order_of(away // (NZ * NY * NC))
    for g in order:
        for cp in loads(g)[1:]:
            cp.wait()
    for i in range(GROUPS):
        for a in range(2):
            halo(a, 1, away_order[i]).start()
            halo(a, 0, order[i]).start()

    row_j = lax.broadcasted_iota(jnp.int32, (HALF, 2 * HALF), 0)
    col_i = lax.broadcasted_iota(jnp.int32, (HALF, 2 * HALF), 1) % HALF
    keep = row_j >= col_i
    first_dev = jnp.where(me == 0, NEG, 0.0).astype(F32)
    last_dev = jnp.where(me == n_seq - 1, NEG, 0.0).astype(F32)
    bias[0] = jnp.where(keep, first_dev, 0.0)
    bias[1] = jnp.where(keep, 0.0, last_dev)
    lane = lax.broadcasted_iota(jnp.int32, (HALF, HALF), 1)
    left = lane < HEAD

    def stacked(t):
        zero = jnp.zeros_like(t)
        return jnp.concatenate([jnp.where(left, t, zero), jnp.where(left, zero, t)], axis=0)

    def diagonal(t):
        return jnp.concatenate([t[:HEAD, :HALF], t[HEAD:, HALF:]], axis=0)

    def block_rows(b):
        return pl.ds(pl.multiple_of(b * HALF, HALF), 3 * HALF)

    def edge_rows(b):
        return pl.ds(pl.multiple_of(b * 3 * HALF, HALF), HALF)

    def ready(g):
        loads(g)[0].wait()
        for p in range(2):
            cb = p * HALF
            for b in range(2):
                rb = b * HALF
                qq = q_s[g, rb:rb + HALF, cb:cb + HALF].astype(F32) * SCALE
                q_st[g, p, b] = stacked(qq).astype(BF)
            v_t[g, p, :, HALF:3 * HALF] = v_s[g, HALF:3 * HALF, cb:cb + HALF].T

    def forward(i, g, p, b):
        cb = p * HALF
        edge = edge_rows(b)
        rr0 = block_rows(b)
        v_t[g, p, :, edge] = v_s[g, edge, cb:cb + HALF].T
        sc = dot(k_s[g, rr0, cb:cb + HALF], q_st[g, p, b], NT)
        mid = sc[HALF:2 * HALF]
        mix = jnp.where(keep, sc[:HALF], sc[2 * HALF:]) + bias[b]
        top = jnp.maximum(jnp.max(mid, axis=0, keepdims=True),
                          jnp.max(mix, axis=0, keepdims=True))
        mid = jnp.exp(mid - top)
        mix = jnp.exp(mix - top)
        total = jnp.sum(mid, axis=0, keepdims=True) + jnp.sum(mix, axis=0, keepdims=True)
        inv = 1.0 / total
        mid = mid * inv
        mix = mix * inv
        pr = jnp.concatenate(
            [jnp.where(keep, mix, 0.0), mid, jnp.where(keep, 0.0, mix)], axis=0).astype(BF)
        p_s[g, p, b] = pr
        att = dot(v_t[g, p, :, rr0], pr)
        a_t[i, :, pl.ds(pl.multiple_of(b * HALF, HALF), HALF)] = diagonal(att).astype(BF)

    def project(slot):
        r = dot(a_t[slot], og[...])
        part[slot] = r.reshape(16, 8, r.shape[1])
        for yy in range(NY):
            t = jnp.concatenate([part[slot, yy * 2 + (1 - c)],
                                 part[slot, 8 + yy * 2 + (1 - c)]], axis=0)
            cs[slot, yy * 16:yy * 16 + 16] = t.astype(BF)
        cp = remote(cs.at[slot], cr.at[slot], csend.at[slot], crecv.at[slot], mate)
        cp.start()
        return cp

    def summed(slot, yy):
        t = jnp.concatenate([part[slot, yy * 2 + c], part[slot, 8 + yy * 2 + c]], axis=0)
        return t + cr[slot, yy * 16:yy * 16 + 16].astype(F32)

    x_dest = [x_far, x_far, x_up, x_dn, x_up, x_dn]
    x_copies = [remote(xs.at[k], xr.at[k], xsend.at[k], xrecv.at[k], x_dest[k]) for k in range(6)]

    def x_fill(slot, extra):
        for yy in range(NY):
            t = summed(slot, yy)
            if extra is not None:
                t = t + xr[extra, yy * 16:yy * 16 + 16].astype(F32)
            xs[slot, yy * 16:yy * 16 + 16] = t.astype(BF)

    def x_send(slot):
        cores[slot].wait_recv()
        if slot < 2:
            x_fill(slot, None)
        else:
            far = 0 if slot < 4 else 1
            adds = c == slot % 2

            @pl.when(adds)
            def _():
                x_copies[far].wait_recv()
                x_fill(slot, far)

            @pl.when(jnp.logical_not(adds))
            def _():
                x_fill(slot, None)

        x_copies[slot].start()

    cores = []
    g_far, g_up, g_dn, g_own = order
    steps = [(0, g_far, 0), (0, g_far, 1), (1, g_up, 0), (2, g_dn, 0),
             (1, g_up, 1), (2, g_dn, 1), (3, g_own, 0), (3, g_own, 1)]
    x_after = {1: [0], 2: [1], 5: [2, 3], 6: [4], 7: [5]}

    def near_step(i):
        place, g, p = steps[i]
        if i in (0, 2, 3, 6):
            ready(g)
            for a in range(2):
                halo(a, 0, g).wait_recv()
        forward(i, g, p, 1 - c)

    def away_step(i):
        place, g, p = steps[i]
        if i in (0, 2, 3, 6):
            for a in range(2):
                halo(a, 1, g).wait_recv()
        forward(i, g, p, c)
        cores.append(project(i))
        for slot in x_after.get(i, []):
            x_send(slot)

    def dattn_of(g):
        d = dot(og[...], w_s[g * GW:(g + 1) * GW, :], NT).astype(BF).astype(F32)
        for p in range(2):
            for b in range(2):
                d_st[g, p, b] = stacked(
                    d[b * HALF:(b + 1) * HALF, p * HALF:(p + 1) * HALF]).astype(BF)

    for i in range(len(steps)):
        near_step(i)
        if i == 1:
            load_og.wait()
            load_w.wait()
        if i % 2:
            dattn_of(i // 2)
    for i in range(len(steps)):
        away_step(i)

    def backward(g, p, side):
        dev, b = sides[side]
        cb = p * HALF
        j = g * 2 + p
        edge = edge_rows(b)
        rr0 = block_rows(b)
        if side == 1:
            k_t[g, p, :, HALF:3 * HALF] = k_s[g, HALF:3 * HALF, cb:cb + HALF].T
        k_t[g, p, :, edge] = k_s[g, edge, cb:cb + HALF].T
        dp = dot(v_s[g, rr0, cb:cb + HALF], d_st[g, p, b], NT)
        pr = p_s[g, p, b]
        prf = pr.astype(F32)
        t = prf * dp
        delta = jnp.sum(t, axis=0, keepdims=True)
        ds = (t - prf * delta).astype(BF)
        own[side, j, 0, rr0] = dot(ds, q_st[g, p, b])
        own[side, j, 1, rr0] = dot(pr, d_st[g, p, b])
        for a in range(2):
            rs[side, j, a] = own[side, j, a, edge].astype(BF)
        cp = remote(rs.at[side, j], rr.at[side, j], rsend.at[side, j], rrecv.at[side, j], dev)
        cp.start()
        dq = diagonal(dot(k_t[g, p, :, rr0], ds)) * SCALE
        qo[pl.ds(pl.multiple_of(b * HALF, HALF), HALF), j * HALF:(j + 1) * HALF] = dq.T.astype(BF)
        return cp

    def finish(j):
        for cp in (near_rims[j], away_rims[j]):
            cp.wait_recv()
        for a, out in enumerate((ko, vo)):
            for side in range(2):
                b = sides[side][1]
                r_in = pl.ds(pl.multiple_of((b + 1) * HALF, HALF), HALF)
                t = own[0, j, a, r_in] + own[1, j, a, r_in] + rr[side, j, a].astype(F32)
                out[pl.ds(pl.multiple_of(b * HALF, HALF), HALF),
                    j * HALF:(j + 1) * HALF] = t.astype(BF)

    quarter = og.shape[1] // (2 * n_dp)
    y_copies = [remote(ysend.at[(y + i) % NY], yrecv.at[i - 1], ysem.at[i - 1],
                       yrsem.at[i - 1], y_to[i - 1]) for i in range(1, NY)]

    def z_copy(to, frm):
        return remote(zs.at[to], zr.at[frm], zsem.at[to], zrsem.at[frm],
                      at(x, to % NZ, y, c), to // NZ)

    def z_stage(p):
        cores[6 + p].wait_recv()
        x_copies[2 + 2 * p].wait_recv()
        x_copies[3 + 2 * p].wait_recv()
        for yy in range(NY):
            r0 = yy * 16
            t = (summed(6 + p, yy) + xr[2 + 2 * p, r0:r0 + 16].astype(F32)
                 + xr[3 + 2 * p, r0:r0 + 16].astype(F32))
            for h in range(2):
                for d in range(n_dp):
                    u = t[h * 8:h * 8 + 8, d * 2 * quarter:(d + 1) * 2 * quarter]
                    u = jnp.concatenate([u[:, :quarter], u[:, quarter:]], axis=0)
                    z_own[d * NZ + p * 2 + h, r0:r0 + 16] = u
                    zs[d * NZ + p * 2 + h, r0:r0 + 16] = u.astype(BF)
        for h in range(2):
            for d in range(n_dp):
                to = d * NZ + p * 2 + h

                @pl.when(z_me != to)
                def _(to=to):
                    z_copy(to, z_me).start()

    def y_stage():
        for z in z_all:
            z_copy(z, z).wait_recv()
        for yy in range(NY):
            r0 = yy * 16
            t = z_own[z_me, r0:r0 + 16]
            for z in z_all:
                t = t + zr[z, r0:r0 + 16].astype(F32)
            y_own[yy] = t
            ysend[yy] = t.astype(BF)
        for cp in y_copies:
            cp.start()

    def y_finish():
        for cp in y_copies:
            cp.wait_recv()
        t = y_own[y]
        for i in range(NY - 1):
            t = t + yrecv[i].astype(F32)
        t = t * ((rows * n_seq * n_dp) ** -0.5)
        wo[:, :quarter] = t[:8]
        wo[:, quarter:] = t[8:]

    away_rims, near_rims = [], []
    for j in range(2 * GROUPS):
        away_rims.append(backward(j // 2, j % 2, 1))
    for j in range(2 * GROUPS):
        near_rims.append(backward(j // 2, j % 2, 0))
        if j == 1:
            z_stage(0)
        elif j == 6:
            z_stage(1)
    y_stage()
    for j in range(2 * GROUPS):
        finish(j)
    y_finish()

    for g in range(GROUPS):
        for a in range(2):
            for side in range(2):
                halo(a, side, g).wait_send()
    for cp in cores + x_copies + y_copies + [z_copy(z, z) for z in z_all]:
        cp.wait_send()
    for cp in away_rims + near_rims:
        cp.wait_send()


def on_device(n_seq, n_dp, queries, keys, values, out_grad, out_weight):
    rows, width = queries.shape[1:]
    half = width // n_dp
    vm = pltpu.VMEM
    dma = pltpu.SemaphoreType.DMA
    nz = NZ * n_dp
    anyspec = pl.BlockSpec(memory_space=pltpu.HBM)
    vspec = pl.BlockSpec(memory_space=pltpu.VMEM)
    scratch = [
        vm((GROUPS, rows, GW), BF), vm((GROUPS, 4 * HALF, GW), BF), vm((GROUPS, 4 * HALF, GW), BF),
        vm((rows, width), BF), vm((width, width), BF),
        vm((GROUPS, 2, HALF, 4 * HALF), BF), vm((GROUPS, 2, HALF, 4 * HALF), BF),
        vm((GROUPS, 2, 2, 2 * HALF, HALF), BF), vm((GROUPS, 2, 2, 2 * HALF, HALF), BF),
        vm((GROUPS, 2, 2, 3 * HALF, 2 * HALF), BF), vm((8, HALF, rows), BF), vm((2, HALF, 2 * HALF), F32),
        vm((8, 16, 8, width), F32), vm((8, HEAD, width), BF), vm((8, HEAD, width), BF),
        vm((6, HEAD, width), BF), vm((6, HEAD, width), BF),
        vm((NY, 16, half // 2), BF), vm((NY - 1, 16, half // 2), BF), vm((NY, 16, half // 2), F32),
        vm((nz, HEAD, half // 2), BF), vm((nz, HEAD, half // 2), BF), vm((nz, HEAD, half // 2), F32),
        vm((2, 8, 2, HALF, HALF), BF), vm((2, 8, 2, HALF, HALF), BF),
        vm((2, 8, 2, 4 * HALF, HALF), F32),
        dma((14,)), dma((2, 2, GROUPS)), dma((2, 2, GROUPS)), dma((8,)), dma((8,)),
        dma((6,)), dma((6,)), dma((NY - 1,)), dma((NY - 1,)), dma((nz,)), dma((nz,)),
        dma((2, 8)), dma((2, 8)),
    ]
    sds = jax.ShapeDtypeStruct
    outs = [sds((3, rows, width), BF), sds((8, half), F32)]
    qkv, wg = pl.pallas_call(
        functools.partial(kernel, n_seq, n_dp),
        out_shape=outs,
        in_specs=[anyspec] * 5,
        out_specs=[vspec] * 2,
        scratch_shapes=scratch,
        compiler_params=pltpu.CompilerParams(
            collective_id=0, has_side_effects=True, vmem_limit_bytes=48 * 1024 * 1024),
    )(*[pltpu.with_memory_space_constraint(t, pltpu.HBM)
        for t in (queries[0], keys[0], values[0], out_grad[0], out_weight)])
    return qkv[0:1], qkv[1:2], qkv[2:3], wg


def solution(mesh):
    n_seq, n_dp = mesh.shape["seq"], mesh.shape["dp"]
    rows = P("dp", "seq", None)
    return jax.shard_map(
        functools.partial(on_device, n_seq, n_dp),
        mesh=mesh,
        in_specs=(rows, rows, rows, rows, P()),
        out_specs=(rows, rows, rows, P("seq", "dp")),
        check_vma=False,
    )
```

```python
import functools

import jax
import jax.numpy as jnp
from jax import lax
from jax.experimental import pallas as pl
from jax.experimental.pallas import tpu as pltpu
from jax.sharding import PartitionSpec as P

HEAD = 64
HALF = 128
BF = jnp.bfloat16
F32 = jnp.float32
NEG = -1e30
NX, NZ, NY, NC = 4, 4, 4, 2
GROUPS = 4
PLAN = ((0, 0), (0, 1), (0, 2), (0, 3), (0, 4), (0, 5), (0, 6), (0, 7),
        (1, 0), (1, 1), (1, 2), (1, 3), (1, 4), (1, 5), (1, 6), (1, 7))
GW = 256
NT = (((1,), (1,)), ((), ()))
NN = (((1,), (0,)), ((), ()))
SCALE = HEAD ** -0.5


def dot(a, b, dims=NN):
    return lax.dot_general(a, b, dims, preferred_element_type=F32)


def kernel(n_seq, n_dp, q_h, k_h, v_h, g_h, w_h, all_o, wo,
           q_s, k_s, v_s, og, w_s, k_t, v_t, q_st, d_st, p_s, a_t, bias,
           part, cs, cr, xs, xr, ysend, yrecv, y_own, zs, zr, z_own, rs, rr, own,
           load_sem, hsend, hrecv, csend, crecv, xsend, xrecv, ysem, yrsem,
           zsem, zrsem, rsend, rrecv):
    me = lax.axis_index("seq")
    zh = lax.axis_index("dp")
    c = me % NC
    y = (me // NC) % NY
    zl = (me // (NC * NY)) % NZ
    x = me // (NC * NY * NZ)
    rows = 2 * HALF
    qo, ko, vo = all_o.at[0], all_o.at[1], all_o.at[2]

    def at(x_, z_, y_, c_):
        return ((x_ * NZ + z_) * NY + y_) * NC + c_

    prev = (me + n_seq - 1) % n_seq
    nxt = (me + 1) % n_seq
    mate = at(x, zl, y, 1 - c)
    x_up = at((x + 1) % NX, zl, y, c)
    x_dn = at((x + NX - 1) % NX, zl, y, c)
    x_far = at((x + 1 + (NX - 2) * c) % NX, zl, y, c)
    y_to = [at(x, zl, (y + i) % NY, c) for i in range(1, NY)]
    z_me = zh * NZ + zl
    z_all = [(z_me + i) % (NZ * n_dp) for i in range(1, NZ * n_dp)]
    z_to = [(at(x, z % NZ, y, c), z // NZ) for z in z_all]

    def remote(src, dst, ss, rsem, seq, dp=None):
        return pltpu.make_async_remote_copy(
            src_ref=src, dst_ref=dst, send_sem=ss, recv_sem=rsem,
            device_id={"seq": seq, "dp": zh if dp is None else dp},
            device_id_type=pl.DeviceIdType.MESH)

    barrier = pltpu.get_barrier_semaphore()
    partners = [(prev, zh), (nxt, zh), (x_up, zh), (x_dn, zh)]
    partners += [(s, zh) for s in y_to] + z_to
    for s, d in partners:
        pl.semaphore_signal(barrier, inc=1, device_id={"seq": s, "dp": d},
                            device_id_type=pl.DeviceIdType.MESH)

    def order_of(x_):
        return [(x_ + 2) % NX, (x_ + 1) % NX, (x_ + 3) % NX, x_]

    order = order_of(x)

    def loads(g):
        cols = pl.ds(pl.multiple_of(g * GW, GW), GW)
        mid = pl.ds(HALF, rows)
        return [pltpu.make_async_copy(q_h.at[:, cols], q_s.at[g], load_sem.at[2 + g]),
                pltpu.make_async_copy(k_h.at[:, cols], k_s.at[g, mid], load_sem.at[6 + g]),
                pltpu.make_async_copy(v_h.at[:, cols], v_s.at[g, mid], load_sem.at[10 + g])]

    load_og = pltpu.make_async_copy(g_h, og, load_sem.at[0])
    load_w = pltpu.make_async_copy(w_h, w_s, load_sem.at[1])
    for i, g in enumerate(order):
        for cp in loads(g):
            cp.start()
        if i == 0:
            load_og.start()
    load_w.start()

    pl.semaphore_wait(barrier, len(partners))

    away = (me + n_seq - 1 + 2 * c) % n_seq
    sides = ((mate, 1 - c), (away, c))

    def halo(a, side, g):
        buf = (k_s, v_s)[a]
        dev, b = sides[side]
        return remote(buf.at[g, pl.ds(pl.multiple_of(HALF * (1 + b), HALF), HALF)],
                      buf.at[g, pl.ds(pl.multiple_of(3 * HALF * (1 - b), HALF), HALF)],
                      hsend.at[a, side, g], hrecv.at[a, side, g], dev)

    away_order = order_of(away // (NZ * NY * NC))
    for g in order:
        for cp in loads(g)[1:]:
            cp.wait()
    for i in range(GROUPS):
        for a in range(2):
            halo(a, 1, away_order[i]).start()
            halo(a, 0, order[i]).start()

    row_j = lax.broadcasted_iota(jnp.int32, (HALF, 2 * HALF), 0)
    col_i = lax.broadcasted_iota(jnp.int32, (HALF, 2 * HALF), 1) % HALF
    keep = row_j >= col_i
    first_dev = jnp.where(me == 0, NEG, 0.0).astype(F32)
    last_dev = jnp.where(me == n_seq - 1, NEG, 0.0).astype(F32)
    bias[0] = jnp.where(keep, first_dev, 0.0)
    bias[1] = jnp.where(keep, 0.0, last_dev)
    lane = lax.broadcasted_iota(jnp.int32, (HALF, HALF), 1)
    left = lane < HEAD

    def stacked(t):
        zero = jnp.zeros_like(t)
        return jnp.concatenate([jnp.where(left, t, zero), jnp.where(left, zero, t)], axis=0)

    def diagonal(t):
        return jnp.concatenate([t[:HEAD, :HALF], t[HEAD:, HALF:]], axis=0)

    def block_rows(b):
        return pl.ds(pl.multiple_of(b * HALF, HALF), 3 * HALF)

    def edge_rows(b):
        return pl.ds(pl.multiple_of(b * 3 * HALF, HALF), HALF)

    def ready(g):
        loads(g)[0].wait()
        for p in range(2):
            cb = p * HALF
            for b in range(2):
                rb = b * HALF
                qq = q_s[g, rb:rb + HALF, cb:cb + HALF].astype(F32) * SCALE
                q_st[g, p, b] = stacked(qq).astype(BF)
            v_t[g, p, :, HALF:3 * HALF] = v_s[g, HALF:3 * HALF, cb:cb + HALF].T

    def forward(i, g, p, b):
        cb = p * HALF
        edge = edge_rows(b)
        rr0 = block_rows(b)
        v_t[g, p, :, edge] = v_s[g, edge, cb:cb + HALF].T
        sc = dot(k_s[g, rr0, cb:cb + HALF], q_st[g, p, b], NT)
        mid = sc[HALF:2 * HALF]
        mix = jnp.where(keep, sc[:HALF], sc[2 * HALF:]) + bias[b]
        top = jnp.maximum(jnp.max(mid, axis=0, keepdims=True),
                          jnp.max(mix, axis=0, keepdims=True))
        mid = jnp.exp(mid - top)
        mix = jnp.exp(mix - top)
        total = jnp.sum(mid, axis=0, keepdims=True) + jnp.sum(mix, axis=0, keepdims=True)
        inv = 1.0 / total
        mid = mid * inv
        mix = mix * inv
        pr = jnp.concatenate(
            [jnp.where(keep, mix, 0.0), mid, jnp.where(keep, 0.0, mix)], axis=0).astype(BF)
        p_s[g, p, b] = pr
        att = dot(v_t[g, p, :, rr0], pr)
        a_t[i, :, pl.ds(pl.multiple_of(b * HALF, HALF), HALF)] = diagonal(att).astype(BF)

    def project(slot):
        r = dot(a_t[slot], og[...])
        part[slot] = r.reshape(16, 8, r.shape[1])
        for yy in range(NY):
            t = jnp.concatenate([part[slot, yy * 2 + (1 - c)],
                                 part[slot, 8 + yy * 2 + (1 - c)]], axis=0)
            cs[slot, yy * 16:yy * 16 + 16] = t.astype(BF)
        cp = remote(cs.at[slot], cr.at[slot], csend.at[slot], crecv.at[slot], mate)
        cp.start()
        return cp

    def summed(slot, yy):
        t = jnp.concatenate([part[slot, yy * 2 + c], part[slot, 8 + yy * 2 + c]], axis=0)
        return t + cr[slot, yy * 16:yy * 16 + 16].astype(F32)

    x_dest = [x_far, x_far, x_up, x_dn, x_up, x_dn]
    x_copies = [remote(xs.at[k], xr.at[k], xsend.at[k], xrecv.at[k], x_dest[k]) for k in range(6)]

    def x_fill(slot, extra):
        for yy in range(NY):
            t = summed(slot, yy)
            if extra is not None:
                t = t + xr[extra, yy * 16:yy * 16 + 16].astype(F32)
            xs[slot, yy * 16:yy * 16 + 16] = t.astype(BF)

    def x_send(slot):
        cores[slot].wait_recv()
        if slot < 2:
            x_fill(slot, None)
        else:
            far = 0 if slot < 4 else 1
            adds = c == slot % 2

            @pl.when(adds)
            def _():
                x_copies[far].wait_recv()
                x_fill(slot, far)

            @pl.when(jnp.logical_not(adds))
            def _():
                x_fill(slot, None)

        x_copies[slot].start()

    cores = []
    g_far, g_up, g_dn, g_own = order
    steps = [(0, g_far, 0), (0, g_far, 1), (1, g_up, 0), (2, g_dn, 0),
             (1, g_up, 1), (2, g_dn, 1), (3, g_own, 0), (3, g_own, 1)]
    x_after = {1: [0], 2: [1], 6: [2, 3], 7: [4, 5]}

    def near_step(i):
        place, g, p = steps[i]
        if i in (0, 2, 3, 6):
            ready(g)
            for a in range(2):
                halo(a, 0, g).wait_recv()
        forward(i, g, p, 1 - c)

    def away_step(i):
        place, g, p = steps[i]
        if i in (0, 2, 3, 6):
            for a in range(2):
                halo(a, 1, g).wait_recv()
        forward(i, g, p, c)
        cores.append(project(i))
        for slot in x_after.get(i, []):
            x_send(slot)

    def dattn_of(g):
        d = dot(og[...], w_s[g * GW:(g + 1) * GW, :], NT).astype(BF).astype(F32)
        for p in range(2):
            for b in range(2):
                d_st[g, p, b] = stacked(
                    d[b * HALF:(b + 1) * HALF, p * HALF:(p + 1) * HALF]).astype(BF)

    def near_all(i):
        near_step(i)
        if i == 1:
            load_og.wait()
            load_w.wait()
        if i % 2:
            dattn_of(i // 2)

    for kind, i in PLAN:
        (near_all, away_step)[kind](i)

    def backward(g, p, side):
        dev, b = sides[side]
        cb = p * HALF
        j = g * 2 + p
        edge = edge_rows(b)
        rr0 = block_rows(b)
        if side == 1:
            k_t[g, p, :, HALF:3 * HALF] = k_s[g, HALF:3 * HALF, cb:cb + HALF].T
        k_t[g, p, :, edge] = k_s[g, edge, cb:cb + HALF].T
        dp = dot(v_s[g, rr0, cb:cb + HALF], d_st[g, p, b], NT)
        pr = p_s[g, p, b]
        prf = pr.astype(F32)
        t = prf * dp
        delta = jnp.sum(t, axis=0, keepdims=True)
        ds = (t - prf * delta).astype(BF)
        own[side, j, 0, rr0] = dot(ds, q_st[g, p, b])
        own[side, j, 1, rr0] = dot(pr, d_st[g, p, b])
        for a in range(2):
            rs[side, j, a] = own[side, j, a, edge].astype(BF)
        cp = remote(rs.at[side, j], rr.at[side, j], rsend.at[side, j], rrecv.at[side, j], dev)
        cp.start()
        dq = diagonal(dot(k_t[g, p, :, rr0], ds)) * SCALE
        qo[pl.ds(pl.multiple_of(b * HALF, HALF), HALF), j * HALF:(j + 1) * HALF] = dq.T.astype(BF)
        return cp

    def finish(j):
        for cp in (near_rims[j], away_rims[j]):
            cp.wait_recv()
        for a, out in enumerate((ko, vo)):
            for side in range(2):
                b = sides[side][1]
                r_in = pl.ds(pl.multiple_of((b + 1) * HALF, HALF), HALF)
                t = own[0, j, a, r_in] + own[1, j, a, r_in] + rr[side, j, a].astype(F32)
                out[pl.ds(pl.multiple_of(b * HALF, HALF), HALF),
                    j * HALF:(j + 1) * HALF] = t.astype(BF)

    quarter = og.shape[1] // (2 * n_dp)
    y_copies = [remote(ysend.at[(y + i) % NY], yrecv.at[i - 1], ysem.at[i - 1],
                       yrsem.at[i - 1], y_to[i - 1]) for i in range(1, NY)]

    def z_copy(to, frm):
        return remote(zs.at[to], zr.at[frm], zsem.at[to], zrsem.at[frm],
                      at(x, to % NZ, y, c), to // NZ)

    def z_stage(p):
        cores[6 + p].wait_recv()
        x_copies[2 + 2 * p].wait_recv()
        x_copies[3 + 2 * p].wait_recv()
        for yy in range(NY):
            r0 = yy * 16
            t = (summed(6 + p, yy) + xr[2 + 2 * p, r0:r0 + 16].astype(F32)
                 + xr[3 + 2 * p, r0:r0 + 16].astype(F32))
            for h in range(2):
                for d in range(n_dp):
                    u = t[h * 8:h * 8 + 8, d * 2 * quarter:(d + 1) * 2 * quarter]
                    u = jnp.concatenate([u[:, :quarter], u[:, quarter:]], axis=0)
                    z_own[d * NZ + p * 2 + h, r0:r0 + 16] = u
                    zs[d * NZ + p * 2 + h, r0:r0 + 16] = u.astype(BF)
        for h in range(2):
            for d in range(n_dp):
                to = d * NZ + p * 2 + h

                @pl.when(z_me != to)
                def _(to=to):
                    z_copy(to, z_me).start()

    def y_stage():
        for z in z_all:
            z_copy(z, z).wait_recv()
        for yy in range(NY):
            r0 = yy * 16
            t = z_own[z_me, r0:r0 + 16]
            for z in z_all:
                t = t + zr[z, r0:r0 + 16].astype(F32)
            y_own[yy] = t
            ysend[yy] = t.astype(BF)
        for cp in y_copies:
            cp.start()

    def y_finish():
        for cp in y_copies:
            cp.wait_recv()
        t = y_own[y]
        for i in range(NY - 1):
            t = t + yrecv[i].astype(F32)
        t = t * ((rows * n_seq * n_dp) ** -0.5)
        wo[:, :quarter] = t[:8]
        wo[:, quarter:] = t[8:]

    away_rims, near_rims = [], []
    for j in range(2 * GROUPS):
        away_rims.append(backward(j // 2, j % 2, 1))
    for j in range(2 * GROUPS):
        near_rims.append(backward(j // 2, j % 2, 0))
        if j == 1:
            z_stage(0)
        elif j == 6:
            z_stage(1)
    y_stage()
    for j in range(2 * GROUPS):
        finish(j)
    y_finish()

    for g in range(GROUPS):
        for a in range(2):
            for side in range(2):
                halo(a, side, g).wait_send()
    for cp in cores + x_copies + y_copies + [z_copy(z, z) for z in z_all]:
        cp.wait_send()
    for cp in away_rims + near_rims:
        cp.wait_send()


def on_device(n_seq, n_dp, queries, keys, values, out_grad, out_weight):
    rows, width = queries.shape[1:]
    half = width // n_dp
    vm = pltpu.VMEM
    dma = pltpu.SemaphoreType.DMA
    nz = NZ * n_dp
    anyspec = pl.BlockSpec(memory_space=pltpu.HBM)
    vspec = pl.BlockSpec(memory_space=pltpu.VMEM)
    scratch = [
        vm((GROUPS, rows, GW), BF), vm((GROUPS, 4 * HALF, GW), BF), vm((GROUPS, 4 * HALF, GW), BF),
        vm((rows, width), BF), vm((width, width), BF),
        vm((GROUPS, 2, HALF, 4 * HALF), BF), vm((GROUPS, 2, HALF, 4 * HALF), BF),
        vm((GROUPS, 2, 2, 2 * HALF, HALF), BF), vm((GROUPS, 2, 2, 2 * HALF, HALF), BF),
        vm((GROUPS, 2, 2, 3 * HALF, 2 * HALF), BF), vm((8, HALF, rows), BF), vm((2, HALF, 2 * HALF), F32),
        vm((8, 16, 8, width), F32), vm((8, HEAD, width), BF), vm((8, HEAD, width), BF),
        vm((6, HEAD, width), BF), vm((6, HEAD, width), BF),
        vm((NY, 16, half // 2), BF), vm((NY - 1, 16, half // 2), BF), vm((NY, 16, half // 2), F32),
        vm((nz, HEAD, half // 2), BF), vm((nz, HEAD, half // 2), BF), vm((nz, HEAD, half // 2), F32),
        vm((2, 8, 2, HALF, HALF), BF), vm((2, 8, 2, HALF, HALF), BF),
        vm((2, 8, 2, 4 * HALF, HALF), F32),
        dma((14,)), dma((2, 2, GROUPS)), dma((2, 2, GROUPS)), dma((8,)), dma((8,)),
        dma((6,)), dma((6,)), dma((NY - 1,)), dma((NY - 1,)), dma((nz,)), dma((nz,)),
        dma((2, 8)), dma((2, 8)),
    ]
    sds = jax.ShapeDtypeStruct
    outs = [sds((3, rows, width), BF), sds((8, half), F32)]
    qkv, wg = pl.pallas_call(
        functools.partial(kernel, n_seq, n_dp),
        out_shape=outs,
        in_specs=[anyspec] * 5,
        out_specs=[vspec] * 2,
        scratch_shapes=scratch,
        compiler_params=pltpu.CompilerParams(
            collective_id=0, has_side_effects=True, vmem_limit_bytes=48 * 1024 * 1024),
    )(*[pltpu.with_memory_space_constraint(t, pltpu.HBM)
        for t in (queries[0], keys[0], values[0], out_grad[0], out_weight)])
    return qkv[0:1], qkv[1:2], qkv[2:3], wg


def solution(mesh):
    n_seq, n_dp = mesh.shape["seq"], mesh.shape["dp"]
    rows = P("dp", "seq", None)
    return jax.shard_map(
        functools.partial(on_device, n_seq, n_dp),
        mesh=mesh,
        in_specs=(rows, rows, rows, rows, P()),
        out_specs=(rows, rows, rows, P("seq", "dp")),
        check_vma=False,
    )
```

```python
import functools

import jax
import jax.numpy as jnp
from jax import lax
from jax.experimental import pallas as pl
from jax.experimental.pallas import tpu as pltpu
from jax.sharding import PartitionSpec as P

HEAD = 64
HALF = 128
BF = jnp.bfloat16
F32 = jnp.float32
NEG = -1e30
NX, NZ, NY, NC = 4, 4, 4, 2
GROUPS = 4
PLAN = ((0, 0), (0, 1), (0, 2), (0, 3), (0, 4), (0, 5), (0, 6), (0, 7),
        (1, 0), (1, 1), (1, 2), (1, 3), (1, 4), (1, 5), (1, 6), (1, 7))
GW = 256
NT = (((1,), (1,)), ((), ()))
NN = (((1,), (0,)), ((), ()))
SCALE = HEAD ** -0.5


def dot(a, b, dims=NN):
    return lax.dot_general(a, b, dims, preferred_element_type=F32)


def kernel(n_seq, n_dp, q_h, k_h, v_h, g_h, w_h, all_o, wo,
           q_s, k_s, v_s, og, w_s, k_t, v_t, q_st, d_st, p_s, a_t, bias,
           part, cs, cr, xs, xr, ysend, yrecv, y_own, zs, zr, z_own, rs, rr, own,
           load_sem, hsend, hrecv, csend, crecv, xsend, xrecv, ysem, yrsem,
           zsem, zrsem, rsend, rrecv):
    me = lax.axis_index("seq")
    zh = lax.axis_index("dp")
    c = me % NC
    y = (me // NC) % NY
    zl = (me // (NC * NY)) % NZ
    x = me // (NC * NY * NZ)
    rows = 2 * HALF
    qo, ko, vo = all_o.at[0], all_o.at[1], all_o.at[2]

    def at(x_, z_, y_, c_):
        return ((x_ * NZ + z_) * NY + y_) * NC + c_

    prev = (me + n_seq - 1) % n_seq
    nxt = (me + 1) % n_seq
    mate = at(x, zl, y, 1 - c)
    x_up = at((x + 1) % NX, zl, y, c)
    x_dn = at((x + NX - 1) % NX, zl, y, c)
    x_far = at((x + 1 + (NX - 2) * c) % NX, zl, y, c)
    y_to = [at(x, zl, (y + i) % NY, c) for i in range(1, NY)]
    z_me = zh * NZ + zl
    z_all = [(z_me + i) % (NZ * n_dp) for i in range(1, NZ * n_dp)]
    z_to = [(at(x, z % NZ, y, c), z // NZ) for z in z_all]

    def remote(src, dst, ss, rsem, seq, dp=None):
        return pltpu.make_async_remote_copy(
            src_ref=src, dst_ref=dst, send_sem=ss, recv_sem=rsem,
            device_id={"seq": seq, "dp": zh if dp is None else dp},
            device_id_type=pl.DeviceIdType.MESH)

    barrier = pltpu.get_barrier_semaphore()
    partners = [(prev, zh), (nxt, zh), (x_up, zh), (x_dn, zh)]
    partners += [(s, zh) for s in y_to] + z_to
    for s, d in partners:
        pl.semaphore_signal(barrier, inc=1, device_id={"seq": s, "dp": d},
                            device_id_type=pl.DeviceIdType.MESH)

    def order_of(x_):
        return [(x_ + 2) % NX, (x_ + 1) % NX, (x_ + 3) % NX, x_]

    order = order_of(x)

    def loads(g):
        cols = pl.ds(pl.multiple_of(g * GW, GW), GW)
        mid = pl.ds(HALF, rows)
        return [pltpu.make_async_copy(q_h.at[:, cols], q_s.at[g], load_sem.at[2 + g]),
                pltpu.make_async_copy(k_h.at[:, cols], k_s.at[g, mid], load_sem.at[6 + g]),
                pltpu.make_async_copy(v_h.at[:, cols], v_s.at[g, mid], load_sem.at[10 + g])]

    load_og = pltpu.make_async_copy(g_h, og, load_sem.at[0])
    load_w = pltpu.make_async_copy(w_h, w_s, load_sem.at[1])
    for i, g in enumerate(order):
        for cp in loads(g):
            cp.start()
        if i == 0:
            load_og.start()
    load_w.start()

    pl.semaphore_wait(barrier, len(partners))

    away = (me + n_seq - 1 + 2 * c) % n_seq
    sides = ((mate, 1 - c), (away, c))

    def halo(a, side, g):
        buf = (k_s, v_s)[a]
        dev, b = sides[side]
        return remote(buf.at[g, pl.ds(pl.multiple_of(HALF * (1 + b), HALF), HALF)],
                      buf.at[g, pl.ds(pl.multiple_of(3 * HALF * (1 - b), HALF), HALF)],
                      hsend.at[a, side, g], hrecv.at[a, side, g], dev)

    away_order = order_of(away // (NZ * NY * NC))
    for g in order:
        for cp in loads(g)[1:]:
            cp.wait()
    for i in range(GROUPS):
        for a in range(2):
            halo(a, 1, away_order[i]).start()
            halo(a, 0, order[i]).start()

    row_j = lax.broadcasted_iota(jnp.int32, (HALF, 2 * HALF), 0)
    col_i = lax.broadcasted_iota(jnp.int32, (HALF, 2 * HALF), 1) % HALF
    keep = row_j >= col_i
    first_dev = jnp.where(me == 0, NEG, 0.0).astype(F32)
    last_dev = jnp.where(me == n_seq - 1, NEG, 0.0).astype(F32)
    bias[0] = jnp.where(keep, first_dev, 0.0)
    bias[1] = jnp.where(keep, 0.0, last_dev)
    lane = lax.broadcasted_iota(jnp.int32, (HALF, HALF), 1)
    left = lane < HEAD

    def stacked(t):
        zero = jnp.zeros_like(t)
        return jnp.concatenate([jnp.where(left, t, zero), jnp.where(left, zero, t)], axis=0)

    def diagonal(t):
        return jnp.concatenate([t[:HEAD, :HALF], t[HEAD:, HALF:]], axis=0)

    def block_rows(b):
        return pl.ds(pl.multiple_of(b * HALF, HALF), 3 * HALF)

    def edge_rows(b):
        return pl.ds(pl.multiple_of(b * 3 * HALF, HALF), HALF)

    def ready(g):
        loads(g)[0].wait()
        for p in range(2):
            cb = p * HALF
            for b in range(2):
                rb = b * HALF
                qq = q_s[g, rb:rb + HALF, cb:cb + HALF].astype(F32) * SCALE
                q_st[g, p, b] = stacked(qq).astype(BF)
            v_t[g, p, :, HALF:3 * HALF] = v_s[g, HALF:3 * HALF, cb:cb + HALF].T

    def forward(i, g, p, b):
        cb = p * HALF
        edge = edge_rows(b)
        rr0 = block_rows(b)
        v_t[g, p, :, edge] = v_s[g, edge, cb:cb + HALF].T
        sc = dot(k_s[g, rr0, cb:cb + HALF], q_st[g, p, b], NT)
        mid = sc[HALF:2 * HALF]
        mix = jnp.where(keep, sc[:HALF], sc[2 * HALF:]) + bias[b]
        top = jnp.maximum(jnp.max(mid, axis=0, keepdims=True),
                          jnp.max(mix, axis=0, keepdims=True))
        mid = jnp.exp(mid - top)
        mix = jnp.exp(mix - top)
        total = jnp.sum(mid, axis=0, keepdims=True) + jnp.sum(mix, axis=0, keepdims=True)
        inv = 1.0 / total
        mid = mid * inv
        mix = mix * inv
        pr = jnp.concatenate(
            [jnp.where(keep, mix, 0.0), mid, jnp.where(keep, 0.0, mix)], axis=0).astype(BF)
        p_s[g, p, b] = pr
        att = dot(v_t[g, p, :, rr0], pr)
        a_t[i, :, pl.ds(pl.multiple_of(b * HALF, HALF), HALF)] = diagonal(att).astype(BF)

    def project(slot):
        r = dot(a_t[slot], og[...])
        part[slot] = r.reshape(16, 8, r.shape[1])
        for yy in range(NY):
            t = jnp.concatenate([part[slot, yy * 2 + (1 - c)],
                                 part[slot, 8 + yy * 2 + (1 - c)]], axis=0)
            cs[slot, yy * 16:yy * 16 + 16] = t.astype(BF)
        cp = remote(cs.at[slot], cr.at[slot], csend.at[slot], crecv.at[slot], mate)
        cp.start()
        return cp

    def summed(slot, yy):
        t = jnp.concatenate([part[slot, yy * 2 + c], part[slot, 8 + yy * 2 + c]], axis=0)
        return t + cr[slot, yy * 16:yy * 16 + 16].astype(F32)

    x_dest = [x_far, x_far, x_up, x_dn, x_up, x_dn]
    x_copies = [remote(xs.at[k], xr.at[k], xsend.at[k], xrecv.at[k], x_dest[k]) for k in range(6)]

    def x_fill(slot, extra):
        for yy in range(NY):
            t = summed(slot, yy)
            if extra is not None:
                t = t + xr[extra, yy * 16:yy * 16 + 16].astype(F32)
            xs[slot, yy * 16:yy * 16 + 16] = t.astype(BF)

    def x_send(slot):
        cores[slot].wait_recv()
        if slot < 2:
            x_fill(slot, None)
        else:
            far = 0 if slot < 4 else 1
            adds = c == slot % 2

            @pl.when(adds)
            def _():
                x_copies[far].wait_recv()
                x_fill(slot, far)

            @pl.when(jnp.logical_not(adds))
            def _():
                x_fill(slot, None)

        x_copies[slot].start()

    cores = []
    g_far, g_up, g_dn, g_own = order
    steps = [(0, g_far, 0), (0, g_far, 1), (1, g_up, 0), (2, g_dn, 0),
             (1, g_up, 1), (2, g_dn, 1), (3, g_own, 0), (3, g_own, 1)]
    x_after = {1: [0], 2: [1], 6: [2, 3], 7: [4, 5]}

    def near_step(i):
        place, g, p = steps[i]
        if i in (0, 2, 3, 6):
            ready(g)
            for a in range(2):
                halo(a, 0, g).wait_recv()
        forward(i, g, p, 1 - c)

    def away_step(i):
        place, g, p = steps[i]
        if i in (0, 2, 3, 6):
            for a in range(2):
                halo(a, 1, g).wait_recv()
        forward(i, g, p, c)
        cores.append(project(i))
        for slot in x_after.get(i, []):
            x_send(slot)

    def dattn_of(g):
        d = dot(og[...], w_s[g * GW:(g + 1) * GW, :], NT).astype(BF).astype(F32)
        for p in range(2):
            for b in range(2):
                d_st[g, p, b] = stacked(
                    d[b * HALF:(b + 1) * HALF, p * HALF:(p + 1) * HALF]).astype(BF)

    def near_all(i):
        near_step(i)
        if i == 1:
            load_og.wait()
            load_w.wait()
        if i % 2:
            dattn_of(i // 2)

    for kind, i in PLAN:
        (near_all, away_step)[kind](i)

    def backward(g, p, side):
        dev, b = sides[side]
        cb = p * HALF
        j = g * 2 + p
        edge = edge_rows(b)
        rr0 = block_rows(b)
        if side == 1:
            k_t[g, p, :, HALF:3 * HALF] = k_s[g, HALF:3 * HALF, cb:cb + HALF].T
        k_t[g, p, :, edge] = k_s[g, edge, cb:cb + HALF].T
        dp = dot(v_s[g, rr0, cb:cb + HALF], d_st[g, p, b], NT)
        pr = p_s[g, p, b]
        prf = pr.astype(F32)
        t = prf * dp
        delta = jnp.sum(t, axis=0, keepdims=True)
        ds = (t - prf * delta).astype(BF)
        own[side, j, 0, rr0] = dot(ds, q_st[g, p, b])
        own[side, j, 1, rr0] = dot(pr, d_st[g, p, b])
        for a in range(2):
            rs[side, j, a] = own[side, j, a, edge].astype(BF)
        cp = remote(rs.at[side, j], rr.at[side, j], rsend.at[side, j], rrecv.at[side, j], dev)
        cp.start()
        dq = diagonal(dot(k_t[g, p, :, rr0], ds)) * SCALE
        qo[pl.ds(pl.multiple_of(b * HALF, HALF), HALF), j * HALF:(j + 1) * HALF] = dq.T.astype(BF)
        return cp

    def finish(j):
        for cp in (near_rims[j], away_rims[j]):
            cp.wait_recv()
        for a, out in enumerate((ko, vo)):
            for side in range(2):
                b = sides[side][1]
                r_in = pl.ds(pl.multiple_of((b + 1) * HALF, HALF), HALF)
                t = own[0, j, a, r_in] + own[1, j, a, r_in] + rr[side, j, a].astype(F32)
                out[pl.ds(pl.multiple_of(b * HALF, HALF), HALF),
                    j * HALF:(j + 1) * HALF] = t.astype(BF)

    quarter = og.shape[1] // (2 * n_dp)
    y_copies = [remote(ysend.at[(y + i) % NY], yrecv.at[i - 1], ysem.at[i - 1],
                       yrsem.at[i - 1], y_to[i - 1]) for i in range(1, NY)]

    def z_copy(to, frm):
        return remote(zs.at[to], zr.at[frm], zsem.at[to], zrsem.at[frm],
                      at(x, to % NZ, y, c), to // NZ)

    def z_stage(p):
        cores[6 + p].wait_recv()
        x_copies[2 + 2 * p].wait_recv()
        x_copies[3 + 2 * p].wait_recv()
        for yy in range(NY):
            r0 = yy * 16
            t = (summed(6 + p, yy) + xr[2 + 2 * p, r0:r0 + 16].astype(F32)
                 + xr[3 + 2 * p, r0:r0 + 16].astype(F32))
            for h in range(2):
                for d in range(n_dp):
                    u = t[h * 8:h * 8 + 8, d * 2 * quarter:(d + 1) * 2 * quarter]
                    u = jnp.concatenate([u[:, :quarter], u[:, quarter:]], axis=0)
                    z_own[d * NZ + p * 2 + h, r0:r0 + 16] = u
                    zs[d * NZ + p * 2 + h, r0:r0 + 16] = u.astype(BF)
        for h in range(2):
            for d in range(n_dp):
                to = d * NZ + p * 2 + h

                @pl.when(z_me != to)
                def _(to=to):
                    z_copy(to, z_me).start()

    def y_stage():
        for z in z_all:
            z_copy(z, z).wait_recv()
        for yy in range(NY):
            r0 = yy * 16
            t = z_own[z_me, r0:r0 + 16]
            for z in z_all:
                t = t + zr[z, r0:r0 + 16].astype(F32)
            y_own[yy] = t
            ysend[yy] = t.astype(BF)
        for cp in y_copies:
            cp.start()

    def y_finish():
        for cp in y_copies:
            cp.wait_recv()
        t = y_own[y]
        for i in range(NY - 1):
            t = t + yrecv[i].astype(F32)
        t = t * ((rows * n_seq * n_dp) ** -0.5)
        wo[:, :quarter] = t[:8]
        wo[:, quarter:] = t[8:]

    away_rims, near_rims = [], []
    for j in range(2 * GROUPS):
        away_rims.append(backward(j // 2, j % 2, 1))
    for j in range(2 * GROUPS):
        near_rims.append(backward(j // 2, j % 2, 0))
        if j == 1:
            z_stage(0)
        elif j == 6:
            z_stage(1)
    for j in range(GROUPS):
        finish(j)
    y_stage()
    for j in range(GROUPS, 2 * GROUPS):
        finish(j)
    y_finish()

    for g in range(GROUPS):
        for a in range(2):
            for side in range(2):
                halo(a, side, g).wait_send()
    for cp in cores + x_copies + y_copies + [z_copy(z, z) for z in z_all]:
        cp.wait_send()
    for cp in away_rims + near_rims:
        cp.wait_send()


def on_device(n_seq, n_dp, queries, keys, values, out_grad, out_weight):
    rows, width = queries.shape[1:]
    half = width // n_dp
    vm = pltpu.VMEM
    dma = pltpu.SemaphoreType.DMA
    nz = NZ * n_dp
    anyspec = pl.BlockSpec(memory_space=pltpu.HBM)
    vspec = pl.BlockSpec(memory_space=pltpu.VMEM)
    scratch = [
        vm((GROUPS, rows, GW), BF), vm((GROUPS, 4 * HALF, GW), BF), vm((GROUPS, 4 * HALF, GW), BF),
        vm((rows, width), BF), vm((width, width), BF),
        vm((GROUPS, 2, HALF, 4 * HALF), BF), vm((GROUPS, 2, HALF, 4 * HALF), BF),
        vm((GROUPS, 2, 2, 2 * HALF, HALF), BF), vm((GROUPS, 2, 2, 2 * HALF, HALF), BF),
        vm((GROUPS, 2, 2, 3 * HALF, 2 * HALF), BF), vm((8, HALF, rows), BF), vm((2, HALF, 2 * HALF), F32),
        vm((8, 16, 8, width), F32), vm((8, HEAD, width), BF), vm((8, HEAD, width), BF),
        vm((6, HEAD, width), BF), vm((6, HEAD, width), BF),
        vm((NY, 16, half // 2), BF), vm((NY - 1, 16, half // 2), BF), vm((NY, 16, half // 2), F32),
        vm((nz, HEAD, half // 2), BF), vm((nz, HEAD, half // 2), BF), vm((nz, HEAD, half // 2), F32),
        vm((2, 8, 2, HALF, HALF), BF), vm((2, 8, 2, HALF, HALF), BF),
        vm((2, 8, 2, 4 * HALF, HALF), F32),
        dma((14,)), dma((2, 2, GROUPS)), dma((2, 2, GROUPS)), dma((8,)), dma((8,)),
        dma((6,)), dma((6,)), dma((NY - 1,)), dma((NY - 1,)), dma((nz,)), dma((nz,)),
        dma((2, 8)), dma((2, 8)),
    ]
    sds = jax.ShapeDtypeStruct
    outs = [sds((3, rows, width), BF), sds((8, half), F32)]
    qkv, wg = pl.pallas_call(
        functools.partial(kernel, n_seq, n_dp),
        out_shape=outs,
        in_specs=[anyspec] * 5,
        out_specs=[vspec] * 2,
        scratch_shapes=scratch,
        compiler_params=pltpu.CompilerParams(
            collective_id=0, has_side_effects=True, vmem_limit_bytes=48 * 1024 * 1024),
    )(*[pltpu.with_memory_space_constraint(t, pltpu.HBM)
        for t in (queries[0], keys[0], values[0], out_grad[0], out_weight)])
    return qkv[0:1], qkv[1:2], qkv[2:3], wg


def solution(mesh):
    n_seq, n_dp = mesh.shape["seq"], mesh.shape["dp"]
    rows = P("dp", "seq", None)
    return jax.shard_map(
        functools.partial(on_device, n_seq, n_dp),
        mesh=mesh,
        in_specs=(rows, rows, rows, rows, P()),
        out_specs=(rows, rows, rows, P("seq", "dp")),
        check_vma=False,
    )
```

```python
import functools

import jax
import jax.numpy as jnp
from jax import lax
from jax.experimental import pallas as pl
from jax.experimental.pallas import tpu as pltpu
from jax.sharding import PartitionSpec as P

HEAD = 64
HALF = 128
BF = jnp.bfloat16
F32 = jnp.float32
NEG = -1e30
NX, NZ, NY, NC = 4, 4, 4, 2
GROUPS = 4
PLAN = ((0, 0), (0, 1), (0, 2), (0, 3), (0, 4), (0, 5), (0, 6), (0, 7),
        (1, 0), (1, 1), (1, 2), (1, 3), (1, 4), (1, 5), (1, 6), (1, 7))
GW = 256
NT = (((1,), (1,)), ((), ()))
NN = (((1,), (0,)), ((), ()))
SCALE = HEAD ** -0.5


def dot(a, b, dims=NN):
    return lax.dot_general(a, b, dims, preferred_element_type=F32)


def kernel(n_seq, n_dp, q_h, k_h, v_h, g_h, w_h, all_o, wo,
           q_s, k_s, v_s, og, w_s, k_t, v_t, q_st, d_st, p_s, a_t, bias,
           part, cs, cr, xs, xr, ysend, yrecv, y_own, zs, zr, z_own, rs, rr, own,
           load_sem, hsend, hrecv, csend, crecv, xsend, xrecv, ysem, yrsem,
           zsem, zrsem, rsend, rrecv):
    me = lax.axis_index("seq")
    zh = lax.axis_index("dp")
    c = me % NC
    y = (me // NC) % NY
    zl = (me // (NC * NY)) % NZ
    x = me // (NC * NY * NZ)
    rows = 2 * HALF
    qo, ko, vo = all_o.at[0], all_o.at[1], all_o.at[2]

    def at(x_, z_, y_, c_):
        return ((x_ * NZ + z_) * NY + y_) * NC + c_

    prev = (me + n_seq - 1) % n_seq
    nxt = (me + 1) % n_seq
    mate = at(x, zl, y, 1 - c)
    x_up = at((x + 1) % NX, zl, y, c)
    x_dn = at((x + NX - 1) % NX, zl, y, c)
    x_far = at((x + 1 + (NX - 2) * c) % NX, zl, y, c)
    y_to = [at(x, zl, (y + i) % NY, c) for i in range(1, NY)]
    z_me = zh * NZ + zl
    z_all = [(z_me + i) % (NZ * n_dp) for i in range(1, NZ * n_dp)]
    z_to = [(at(x, z % NZ, y, c), z // NZ) for z in z_all]

    def remote(src, dst, ss, rsem, seq, dp=None):
        return pltpu.make_async_remote_copy(
            src_ref=src, dst_ref=dst, send_sem=ss, recv_sem=rsem,
            device_id={"seq": seq, "dp": zh if dp is None else dp},
            device_id_type=pl.DeviceIdType.MESH)

    barrier = pltpu.get_barrier_semaphore()
    partners = [(prev, zh), (nxt, zh), (x_up, zh), (x_dn, zh)]
    partners += [(s, zh) for s in y_to] + z_to
    for s, d in partners:
        pl.semaphore_signal(barrier, inc=1, device_id={"seq": s, "dp": d},
                            device_id_type=pl.DeviceIdType.MESH)

    def order_of(x_):
        return [(x_ + 2) % NX, (x_ + 1) % NX, (x_ + 3) % NX, x_]

    order = order_of(x)

    def loads(g):
        cols = pl.ds(pl.multiple_of(g * GW, GW), GW)
        mid = pl.ds(HALF, rows)
        return [pltpu.make_async_copy(q_h.at[:, cols], q_s.at[g], load_sem.at[2 + g]),
                pltpu.make_async_copy(k_h.at[:, cols], k_s.at[g, mid], load_sem.at[6 + g]),
                pltpu.make_async_copy(v_h.at[:, cols], v_s.at[g, mid], load_sem.at[10 + g])]

    load_og = pltpu.make_async_copy(g_h, og, load_sem.at[0])
    load_w = pltpu.make_async_copy(w_h, w_s, load_sem.at[1])
    for i, g in enumerate(order):
        for cp in loads(g):
            cp.start()
        if i == 0:
            load_og.start()
    load_w.start()

    pl.semaphore_wait(barrier, len(partners))

    away = (me + n_seq - 1 + 2 * c) % n_seq
    sides = ((mate, 1 - c), (away, c))

    def halo(a, side, g):
        buf = (k_s, v_s)[a]
        dev, b = sides[side]
        return remote(buf.at[g, pl.ds(pl.multiple_of(HALF * (1 + b), HALF), HALF)],
                      buf.at[g, pl.ds(pl.multiple_of(3 * HALF * (1 - b), HALF), HALF)],
                      hsend.at[a, side, g], hrecv.at[a, side, g], dev)

    away_order = order_of(away // (NZ * NY * NC))
    for g in order:
        for cp in loads(g)[1:]:
            cp.wait()
    for i in range(GROUPS):
        for a in range(2):
            halo(a, 1, away_order[i]).start()
    for i in range(GROUPS):
        for a in range(2):
            halo(a, 0, order[i]).start()

    row_j = lax.broadcasted_iota(jnp.int32, (HALF, 2 * HALF), 0)
    col_i = lax.broadcasted_iota(jnp.int32, (HALF, 2 * HALF), 1) % HALF
    keep = row_j >= col_i
    first_dev = jnp.where(me == 0, NEG, 0.0).astype(F32)
    last_dev = jnp.where(me == n_seq - 1, NEG, 0.0).astype(F32)
    bias[0] = jnp.where(keep, first_dev, 0.0)
    bias[1] = jnp.where(keep, 0.0, last_dev)
    lane = lax.broadcasted_iota(jnp.int32, (HALF, HALF), 1)
    left = lane < HEAD

    def stacked(t):
        zero = jnp.zeros_like(t)
        return jnp.concatenate([jnp.where(left, t, zero), jnp.where(left, zero, t)], axis=0)

    def diagonal(t):
        return jnp.concatenate([t[:HEAD, :HALF], t[HEAD:, HALF:]], axis=0)

    def block_rows(b):
        return pl.ds(pl.multiple_of(b * HALF, HALF), 3 * HALF)

    def edge_rows(b):
        return pl.ds(pl.multiple_of(b * 3 * HALF, HALF), HALF)

    def ready(g):
        loads(g)[0].wait()
        for p in range(2):
            cb = p * HALF
            for b in range(2):
                rb = b * HALF
                qq = q_s[g, rb:rb + HALF, cb:cb + HALF].astype(F32) * SCALE
                q_st[g, p, b] = stacked(qq).astype(BF)
            v_t[g, p, :, HALF:3 * HALF] = v_s[g, HALF:3 * HALF, cb:cb + HALF].T

    def forward(i, g, p, b):
        cb = p * HALF
        edge = edge_rows(b)
        rr0 = block_rows(b)
        v_t[g, p, :, edge] = v_s[g, edge, cb:cb + HALF].T
        sc = dot(k_s[g, rr0, cb:cb + HALF], q_st[g, p, b], NT)
        mid = sc[HALF:2 * HALF]
        mix = jnp.where(keep, sc[:HALF], sc[2 * HALF:]) + bias[b]
        top = jnp.maximum(jnp.max(mid, axis=0, keepdims=True),
                          jnp.max(mix, axis=0, keepdims=True))
        mid = jnp.exp(mid - top)
        mix = jnp.exp(mix - top)
        total = jnp.sum(mid, axis=0, keepdims=True) + jnp.sum(mix, axis=0, keepdims=True)
        inv = 1.0 / total
        mid = mid * inv
        mix = mix * inv
        pr = jnp.concatenate(
            [jnp.where(keep, mix, 0.0), mid, jnp.where(keep, 0.0, mix)], axis=0).astype(BF)
        p_s[g, p, b] = pr
        att = dot(v_t[g, p, :, rr0], pr)
        a_t[i, :, pl.ds(pl.multiple_of(b * HALF, HALF), HALF)] = diagonal(att).astype(BF)

    def project(slot):
        r = dot(a_t[slot], og[...])
        part[slot] = r.reshape(16, 8, r.shape[1])
        for yy in range(NY):
            t = jnp.concatenate([part[slot, yy * 2 + (1 - c)],
                                 part[slot, 8 + yy * 2 + (1 - c)]], axis=0)
            cs[slot, yy * 16:yy * 16 + 16] = t.astype(BF)
        cp = remote(cs.at[slot], cr.at[slot], csend.at[slot], crecv.at[slot], mate)
        cp.start()
        return cp

    def summed(slot, yy):
        t = jnp.concatenate([part[slot, yy * 2 + c], part[slot, 8 + yy * 2 + c]], axis=0)
        return t + cr[slot, yy * 16:yy * 16 + 16].astype(F32)

    x_dest = [x_far, x_far, x_up, x_dn, x_up, x_dn]
    x_copies = [remote(xs.at[k], xr.at[k], xsend.at[k], xrecv.at[k], x_dest[k]) for k in range(6)]

    def x_fill(slot, extra):
        for yy in range(NY):
            t = summed(slot, yy)
            if extra is not None:
                t = t + xr[extra, yy * 16:yy * 16 + 16].astype(F32)
            xs[slot, yy * 16:yy * 16 + 16] = t.astype(BF)

    def x_send(slot):
        cores[slot].wait_recv()
        if slot < 2:
            x_fill(slot, None)
        else:
            far = 0 if slot < 4 else 1
            adds = c == slot % 2

            @pl.when(adds)
            def _():
                x_copies[far].wait_recv()
                x_fill(slot, far)

            @pl.when(jnp.logical_not(adds))
            def _():
                x_fill(slot, None)

        x_copies[slot].start()

    cores = []
    g_far, g_up, g_dn, g_own = order
    steps = [(0, g_far, 0), (0, g_far, 1), (1, g_up, 0), (2, g_dn, 0),
             (1, g_up, 1), (2, g_dn, 1), (3, g_own, 0), (3, g_own, 1)]
    x_after = {1: [0], 2: [1], 6: [2, 3], 7: [4, 5]}

    def near_step(i):
        place, g, p = steps[i]
        if i in (0, 2, 3, 6):
            ready(g)
            for a in range(2):
                halo(a, 0, g).wait_recv()
        forward(i, g, p, 1 - c)

    def away_step(i):
        place, g, p = steps[i]
        if i in (0, 2, 3, 6):
            for a in range(2):
                halo(a, 1, g).wait_recv()
        forward(i, g, p, c)
        cores.append(project(i))
        for slot in x_after.get(i, []):
            x_send(slot)

    def dattn_of(g):
        d = dot(og[...], w_s[g * GW:(g + 1) * GW, :], NT).astype(BF).astype(F32)
        for p in range(2):
            for b in range(2):
                d_st[g, p, b] = stacked(
                    d[b * HALF:(b + 1) * HALF, p * HALF:(p + 1) * HALF]).astype(BF)

    def near_all(i):
        near_step(i)
        if i == 1:
            load_og.wait()
            load_w.wait()
        if i % 2:
            dattn_of(i // 2)

    for kind, i in PLAN:
        (near_all, away_step)[kind](i)

    def backward(g, p, side):
        dev, b = sides[side]
        cb = p * HALF
        j = g * 2 + p
        edge = edge_rows(b)
        rr0 = block_rows(b)
        if side == 1:
            k_t[g, p, :, HALF:3 * HALF] = k_s[g, HALF:3 * HALF, cb:cb + HALF].T
        k_t[g, p, :, edge] = k_s[g, edge, cb:cb + HALF].T
        dp = dot(v_s[g, rr0, cb:cb + HALF], d_st[g, p, b], NT)
        pr = p_s[g, p, b]
        prf = pr.astype(F32)
        t = prf * dp
        delta = jnp.sum(t, axis=0, keepdims=True)
        ds = (t - prf * delta).astype(BF)
        own[side, j, 0, rr0] = dot(ds, q_st[g, p, b])
        own[side, j, 1, rr0] = dot(pr, d_st[g, p, b])
        for a in range(2):
            rs[side, j, a] = own[side, j, a, edge].astype(BF)
        cp = remote(rs.at[side, j], rr.at[side, j], rsend.at[side, j], rrecv.at[side, j], dev)
        cp.start()
        dq = diagonal(dot(k_t[g, p, :, rr0], ds)) * SCALE
        qo[pl.ds(pl.multiple_of(b * HALF, HALF), HALF), j * HALF:(j + 1) * HALF] = dq.T.astype(BF)
        return cp

    def finish(j):
        for cp in (near_rims[j], away_rims[j]):
            cp.wait_recv()
        for a, out in enumerate((ko, vo)):
            for side in range(2):
                b = sides[side][1]
                r_in = pl.ds(pl.multiple_of((b + 1) * HALF, HALF), HALF)
                t = own[0, j, a, r_in] + own[1, j, a, r_in] + rr[side, j, a].astype(F32)
                out[pl.ds(pl.multiple_of(b * HALF, HALF), HALF),
                    j * HALF:(j + 1) * HALF] = t.astype(BF)

    quarter = og.shape[1] // (2 * n_dp)
    y_copies = [remote(ysend.at[(y + i) % NY], yrecv.at[i - 1], ysem.at[i - 1],
                       yrsem.at[i - 1], y_to[i - 1]) for i in range(1, NY)]

    def z_copy(to, frm):
        return remote(zs.at[to], zr.at[frm], zsem.at[to], zrsem.at[frm],
                      at(x, to % NZ, y, c), to // NZ)

    def z_stage(p):
        cores[6 + p].wait_recv()
        x_copies[2 + 2 * p].wait_recv()
        x_copies[3 + 2 * p].wait_recv()
        for yy in range(NY):
            r0 = yy * 16
            t = (summed(6 + p, yy) + xr[2 + 2 * p, r0:r0 + 16].astype(F32)
                 + xr[3 + 2 * p, r0:r0 + 16].astype(F32))
            for h in range(2):
                for d in range(n_dp):
                    u = t[h * 8:h * 8 + 8, d * 2 * quarter:(d + 1) * 2 * quarter]
                    u = jnp.concatenate([u[:, :quarter], u[:, quarter:]], axis=0)
                    z_own[d * NZ + p * 2 + h, r0:r0 + 16] = u
                    zs[d * NZ + p * 2 + h, r0:r0 + 16] = u.astype(BF)
        for h in range(2):
            for d in range(n_dp):
                to = d * NZ + p * 2 + h

                @pl.when(z_me != to)
                def _(to=to):
                    z_copy(to, z_me).start()

    def y_stage():
        for z in z_all:
            z_copy(z, z).wait_recv()
        for yy in range(NY):
            r0 = yy * 16
            t = z_own[z_me, r0:r0 + 16]
            for z in z_all:
                t = t + zr[z, r0:r0 + 16].astype(F32)
            y_own[yy] = t
            ysend[yy] = t.astype(BF)
        for cp in y_copies:
            cp.start()

    def y_finish():
        for cp in y_copies:
            cp.wait_recv()
        t = y_own[y]
        for i in range(NY - 1):
            t = t + yrecv[i].astype(F32)
        t = t * ((rows * n_seq * n_dp) ** -0.5)
        wo[:, :quarter] = t[:8]
        wo[:, quarter:] = t[8:]

    away_rims, near_rims = [], []
    for j in range(2 * GROUPS):
        away_rims.append(backward(j // 2, j % 2, 1))
    for j in range(2 * GROUPS):
        near_rims.append(backward(j // 2, j % 2, 0))
        if j == 1:
            z_stage(0)
        elif j == 6:
            z_stage(1)
    y_stage()
    for j in range(2 * GROUPS):
        finish(j)
    y_finish()

    for g in range(GROUPS):
        for a in range(2):
            for side in range(2):
                halo(a, side, g).wait_send()
    for cp in cores + x_copies + y_copies + [z_copy(z, z) for z in z_all]:
        cp.wait_send()
    for cp in away_rims + near_rims:
        cp.wait_send()


def on_device(n_seq, n_dp, queries, keys, values, out_grad, out_weight):
    rows, width = queries.shape[1:]
    half = width // n_dp
    vm = pltpu.VMEM
    dma = pltpu.SemaphoreType.DMA
    nz = NZ * n_dp
    anyspec = pl.BlockSpec(memory_space=pltpu.HBM)
    vspec = pl.BlockSpec(memory_space=pltpu.VMEM)
    scratch = [
        vm((GROUPS, rows, GW), BF), vm((GROUPS, 4 * HALF, GW), BF), vm((GROUPS, 4 * HALF, GW), BF),
        vm((rows, width), BF), vm((width, width), BF),
        vm((GROUPS, 2, HALF, 4 * HALF), BF), vm((GROUPS, 2, HALF, 4 * HALF), BF),
        vm((GROUPS, 2, 2, 2 * HALF, HALF), BF), vm((GROUPS, 2, 2, 2 * HALF, HALF), BF),
        vm((GROUPS, 2, 2, 3 * HALF, 2 * HALF), BF), vm((8, HALF, rows), BF), vm((2, HALF, 2 * HALF), F32),
        vm((8, 16, 8, width), F32), vm((8, HEAD, width), BF), vm((8, HEAD, width), BF),
        vm((6, HEAD, width), BF), vm((6, HEAD, width), BF),
        vm((NY, 16, half // 2), BF), vm((NY - 1, 16, half // 2), BF), vm((NY, 16, half // 2), F32),
        vm((nz, HEAD, half // 2), BF), vm((nz, HEAD, half // 2), BF), vm((nz, HEAD, half // 2), F32),
        vm((2, 8, 2, HALF, HALF), BF), vm((2, 8, 2, HALF, HALF), BF),
        vm((2, 8, 2, 4 * HALF, HALF), F32),
        dma((14,)), dma((2, 2, GROUPS)), dma((2, 2, GROUPS)), dma((8,)), dma((8,)),
        dma((6,)), dma((6,)), dma((NY - 1,)), dma((NY - 1,)), dma((nz,)), dma((nz,)),
        dma((2, 8)), dma((2, 8)),
    ]
    sds = jax.ShapeDtypeStruct
    outs = [sds((3, rows, width), BF), sds((8, half), F32)]
    qkv, wg = pl.pallas_call(
        functools.partial(kernel, n_seq, n_dp),
        out_shape=outs,
        in_specs=[anyspec] * 5,
        out_specs=[vspec] * 2,
        scratch_shapes=scratch,
        compiler_params=pltpu.CompilerParams(
            collective_id=0, has_side_effects=True, vmem_limit_bytes=48 * 1024 * 1024),
    )(*[pltpu.with_memory_space_constraint(t, pltpu.HBM)
        for t in (queries[0], keys[0], values[0], out_grad[0], out_weight)])
    return qkv[0:1], qkv[1:2], qkv[2:3], wg


def solution(mesh):
    n_seq, n_dp = mesh.shape["seq"], mesh.shape["dp"]
    rows = P("dp", "seq", None)
    return jax.shard_map(
        functools.partial(on_device, n_seq, n_dp),
        mesh=mesh,
        in_specs=(rows, rows, rows, rows, P()),
        out_specs=(rows, rows, rows, P("seq", "dp")),
        check_vma=False,
    )
```
